256 devices in a mesh: sec: 64 (over x, z, core), env: 4 (over y).
Axes of the slice: x: 4, y: 4, z: 8, core: 2. Of those that a mesh axis runs over, the one named last changes fastest.
Arguments:
- wavefunction: float32 [256, 256, 256], P('sec', 'env'), as said below
- left_env: bfloat16 [256, 16, 256, 256], P('sec', None, 'env'), may hold values from -0.375 to 0.375
- right_env: bfloat16 [256, 16, 256, 256], P('sec'), may hold values from -0.375 to 0.375
- shifts: int32 [16], replicated, may hold values from -2 to 2, as said below
- block_dims: int32 [256, 2], P('sec'), may hold values from 128 to 256, as said below
- precond: float32 [256, 256], P('sec', 'env'), may hold values from 0.5 to 4
Outputs:
- ritz_vector: float32 [256, 256, 256], P('sec', 'env')
- ritz_values: float32 [2], replicated
The draws below stay inside these ranges and needn't reach their ends.
Inputs may be any that keep to these rules, and one draw needn't show every extreme that they name: Term w of sector s reads the block of sector s + shifts[w]. `block_dims`: entries of a block beyond these dimensions are padding. `wavefunction`: a real field; sectors differ in scale.
All inputs are finite; a program needn't handle non-finite values.
Results may differ from the reference program's by a relative error of at most 0.0041.
Values may be sent and summed in bfloat16 or wider, within the bound.
A program may use at most 64 MiB of HBM per device.

```python
import math
import jax
import jax.numpy as jnp
from jax import lax

B = 256
W = 16
MAXSHIFT = 2
ITERS = 2
SECTORS = 256


def draw_wavefunction(key, part):
    key = jax.random.fold_in(key, 11)
    key_base, key_rows = jax.random.split(key, 2)
    base = jax.random.normal(key_base, (SECTORS, B, B), jnp.float32)
    sector_scale = 1.0 + 2.0 * jnp.arange(SECTORS, dtype=jnp.float32) / max(SECTORS - 1, 1)
    row_scale = jnp.exp(jax.random.uniform(key_rows, (SECTORS, B, 1), jnp.float32, -0.7, 0.7))
    return base * sector_scale[:, None, None] * row_scale


def draw_shifts(key, part):
    key = jax.random.fold_in(key, 5)
    values = jax.random.randint(key, (W,), -MAXSHIFT, MAXSHIFT + 1, jnp.int32)
    return values.at[0].set(MAXSHIFT).at[1].set(-MAXSHIFT)


def draw_block_dims(key, part):
    key = jax.random.fold_in(key, 7)
    values = jax.random.randint(key, (SECTORS, 2), B // 2, B + 1, jnp.int32)
    return values.at[0].set(B).at[1].set(B // 2)


def levels(key, shape, cuts, least, largest):
    loudness, own = 1.0, jax.random.fold_in(key, 6)
    for position, blocks in cuts:
        steps = jnp.exp(jax.random.uniform(jax.random.fold_in(own, position), (blocks,), jnp.float32, least / len(cuts), largest / len(cuts)))
        loudness = loudness * jnp.repeat(steps, shape[position] // blocks).reshape([-1 if axis == position else 1 for axis in range(len(shape))])
    return loudness


def bell_draw(stream_key, shape, scale, reach, cuts=(), kind=jnp.bfloat16):
    values = scale * jax.random.normal(stream_key, shape, jnp.float32)
    if cuts:
        values = values * levels(stream_key, shape, cuts, -0.22, 0.18)
    return jnp.clip(values, -reach, reach).astype(kind)


def setup_inputs(seed: int = 0) -> dict:
    splits = jax.random.split(jax.random.key(seed), 7)
    wavefunction = draw_wavefunction(jax.random.fold_in(splits[6], 71), 0)
    left_env = bell_draw(splits[1], (SECTORS, W, B, B), B ** -0.5, 0.375, ((0, 64), (2, 4)))
    right_env = bell_draw(splits[2], (SECTORS, W, B, B), B ** -0.5, 0.375, ((0, 64),))
    shifts = draw_shifts(jax.random.fold_in(splits[6], 71), 0)
    block_dims = draw_block_dims(jax.random.fold_in(splits[6], 71), 0)
    precond = jnp.clip(jnp.exp(math.log(4.0) - 2.0794415 * jax.random.uniform(splits[5], (SECTORS, B), jnp.float32) ** levels(splits[5], (SECTORS, B), ((0, 64), (1, 4)), -0.2, 0.2)), 0.5, 4.0)
    return dict(wavefunction=wavefunction, left_env=left_env, right_env=right_env, shifts=shifts, block_dims=block_dims, precond=precond)


def mean_product(first, second):
    return jnp.sum(first * second) / (SECTORS * B * B)

def apply_hamiltonian(vector, left_env, right_env, shifts, live):
    narrow = lax.optimization_barrier(vector.astype(jnp.bfloat16))
    zero_rim = jnp.zeros((MAXSHIFT, B, B), jnp.bfloat16)
    widened = jnp.concatenate([zero_rim, narrow, zero_rim], axis=0)
    total = jnp.zeros((SECTORS, B, B), jnp.float32)
    for term_no in range(W):
        start_at = (shifts[term_no] + MAXSHIFT).astype(jnp.int32)
        source = lax.dynamic_slice_in_dim(widened, start_at, SECTORS, 0)
        partial_rows = jnp.einsum('sij,sjk->sik', left_env[:, term_no].astype(jnp.float32), source.astype(jnp.float32))
        partial_rows = lax.optimization_barrier(partial_rows.astype(jnp.bfloat16))
        total = total + jnp.einsum('sij,sjk->sik', partial_rows.astype(jnp.float32), right_env[:, term_no].astype(jnp.float32))
    return total * live

def reference(wavefunction, left_env, right_env, shifts, block_dims, precond):
    row_ids = jnp.arange(B, dtype=jnp.int32)
    rows_ok = row_ids[None, :] < block_dims[:, 0:1]
    cols_ok = row_ids[None, :] < block_dims[:, 1:2]
    live = (rows_ok[:, :, None] & cols_ok[:, None, :]).astype(jnp.float32)
    start = wavefunction * live
    vector = start * lax.rsqrt(mean_product(start, start) + 1e-06)
    applied = apply_hamiltonian(vector, left_env, right_env, shifts, live)
    values = []
    for step in range(ITERS):
        rayleigh = mean_product(vector, applied)
        correction = (applied - rayleigh * vector) / precond[:, :, None]
        correction = correction - mean_product(vector, correction) * vector
        unit = correction * lax.rsqrt(mean_product(correction, correction) + 1e-06)
        applied_unit = apply_hamiltonian(unit, left_env, right_env, shifts, live)
        coupling = 0.5 * (mean_product(unit, applied) + mean_product(vector, applied_unit))
        upper = mean_product(unit, applied_unit)
        angle = 0.5 * jnp.arctan2(-2.0 * coupling, upper - rayleigh)
        values.append(0.5 * (rayleigh + upper) - jnp.sqrt(0.25 * (rayleigh - upper) ** 2 + coupling ** 2))
        cosine = jnp.cos(angle)
        sine_t = jnp.sin(angle)
        vector = cosine * vector + sine_t * unit
        applied = cosine * applied + sine_t * applied_unit
    return (vector, jnp.stack(values).astype(jnp.float32))
```

```python
import jax
import jax.numpy as jnp
from jax import lax
from jax.experimental import pallas as pl
from jax.experimental.pallas import tpu as pltpu
from jax.sharding import PartitionSpec as P

MAXSHIFT = 2
BF = jnp.bfloat16
F32 = jnp.float32
MESH = pl.DeviceIdType.MESH
ENV = 4
LANES = 128


def dot(a, b):
    return jnp.dot(a, b, preferred_element_type=F32)


def make_kernel(nsec, sectors, terms, rows, cols):
    zs = 8 if nsec % 16 == 0 else 2
    xs = nsec // (2 * zs)
    near = 2 * ENV * xs
    wide = sectors + 2 * MAXSHIFT
    count = float(nsec * sectors * ENV * rows * cols)

    def kernel(
        shifts, dims, wf, prec, left_hbm, right_hbm, out, ritz,
        left, right, xs_buf, xd_buf, xq_buf, xt_buf, dall, dpad, dcol, dinv,
        live, start, va, vda, vh, vq, vc, near_slots, far_slots, total,
        load_sem, go_sem, gi_sem, out_sem, in_sem, send_sem, d_send, d_recv,
        near_send, near_recv, far_send, far_recv,
    ):
        sec = lax.axis_index("sec")
        y = lax.axis_index("env")
        core = lax.rem(sec, 2)
        chip = sec // 2
        z = lax.rem(chip, zs)
        x = chip // zs
        has_out = jnp.logical_or(
            jnp.logical_and(core == 0, sec > 0), jnp.logical_and(core == 1, sec < nsec - 1)
        )
        outer = jnp.clip(sec + 2 * core - 1, 0, nsec - 1)
        inner = sec + 1 - 2 * core
        out_src, out_dst = 2 * core, 6 * (1 - core)
        in_src, in_dst = 2 * (1 - core), 6 * core

        def yy(k):
            return lax.rem(y + k + ENV, ENV)

        near_rank = (core * ENV + y) * xs + x

        def near_peer(k):
            m = lax.rem(near_rank + k, near)
            return (((lax.rem(m, xs) * zs + z) * 2 + m // (xs * ENV)), lax.rem(m // xs, ENV))

        def far_peer(k):
            m = lax.rem(z + k, zs)
            return (((x * zs + m) * 2 + core), y)

        load_left = pltpu.make_async_copy(left_hbm, left, load_sem.at[0])
        load_right = pltpu.make_async_copy(right_hbm, right, load_sem.at[1])
        load_left.start()
        load_right.start()

        zero = jnp.zeros((MAXSHIFT, ENV, rows, cols), BF)
        ones = jnp.ones((MAXSHIFT, ENV, 1, LANES), F32)

        @pl.when(sec == 0)
        def _():
            for buf in (xs_buf, xd_buf, xq_buf):
                buf[0:MAXSHIFT] = zero
            dall[0:MAXSHIFT] = ones

        @pl.when(sec == nsec - 1)
        def _():
            for buf in (xs_buf, xd_buf, xq_buf):
                buf[wide - MAXSHIFT : wide] = zero
            dall[wide - MAXSHIFT : wide] = ones

        barrier = pltpu.get_barrier_semaphore()
        for k in range(1, near):
            pl.semaphore_signal(barrier, inc=1, device_id=near_peer(k), device_id_type=MESH)
        for k in range(1, zs):
            pl.semaphore_signal(barrier, inc=1, device_id=far_peer(k), device_id_type=MESH)

        @pl.when(has_out)
        def _():
            for k in range(ENV):
                pl.semaphore_signal(barrier, inc=1, device_id=(outer, yy(k)), device_id_type=MESH)

        row_ids = y * rows + lax.broadcasted_iota(jnp.int32, (rows, cols), 0)
        col_ids = lax.broadcasted_iota(jnp.int32, (rows, cols), 1)
        own = pl.ds(MAXSHIFT, sectors)
        sq = jnp.zeros((rows, cols), F32)
        for s in range(sectors):
            ok = jnp.logical_and(row_ids < dims[s, 0], col_ids < dims[s, 1])
            mask = jnp.where(ok, 1.0, 0.0).astype(F32)
            live[s] = mask
            st = wf[s] * mask
            start[s] = st
            xs_buf[MAXSHIFT + s, y] = st.astype(BF)
            sq = sq + st * st
            dall[MAXSHIFT + s, y, :, 0:rows] = prec[s : s + 1, :]

        def fold(v):
            w = jnp.sum(v.reshape(rows // 8, 8, cols), axis=0)
            t = w[:, 0:LANES]
            for c in range(1, cols // LANES):
                t = t + w[:, c * LANES : (c + 1) * LANES]
            return jnp.sum(t, axis=0, keepdims=True)

        pl.semaphore_wait(barrier, near - 1 + zs - 1 + jnp.where(has_out, ENV, 0))

        def cp(src, dst, ss, rs, dev):
            return pltpu.make_async_remote_copy(
                src_ref=src, dst_ref=dst, send_sem=ss, recv_sem=rs, device_id=dev, device_id_type=MESH
            )

        ORDER = (1, 3, 2)

        def gather_outer(e, buf, k):
            part = buf.at[pl.ds(MAXSHIFT + out_src, 2), y]
            return cp(part, part, send_sem.at[e, 0, k], go_sem.at[e, k], (sec, yy(k)))

        def gather_inner(e, buf, k):
            part = buf.at[pl.ds(MAXSHIFT + in_src, 2), y]
            return cp(part, part, send_sem.at[e, 1, k], gi_sem.at[e, k], (sec, yy(k)))

        def relay_outer(e, buf, k):
            p = yy(-k)
            src = buf.at[pl.ds(MAXSHIFT + out_src, 2), p]
            dst = buf.at[pl.ds(out_dst, 2), p]
            return cp(src, dst, send_sem.at[e, 2, k], out_sem.at[e, k], (outer, y))

        def relay_inner(e, buf, k):
            p = yy(-k)
            src = buf.at[pl.ds(MAXSHIFT + in_src, 2), p]
            dst = buf.at[pl.ds(in_dst, 2), p]
            return cp(src, dst, send_sem.at[e, 3, k], in_sem.at[e, k], (inner, y))

        def begin(e, buf):
            @pl.when(has_out)
            def _():
                relay_outer(e, buf, 0).start()

            for k in ORDER:
                gather_outer(e, buf, k).start()
            relay_inner(e, buf, 0).start()
            for k in ORDER:
                gather_inner(e, buf, k).start()

        def relay(e, buf):
            for k in ORDER:
                gather_outer(e, buf, k).wait_recv()

                @pl.when(has_out)
                def _():
                    relay_outer(e, buf, k).start()

            for k in ORDER:
                gather_inner(e, buf, k).wait_recv()
                relay_inner(e, buf, k).start()

        def finish(e, buf):
            for k in (0,) + ORDER:
                relay_inner(e, buf, k).wait_recv()

            @pl.when(has_out)
            def _():
                for k in (0,) + ORDER:
                    relay_outer(e, buf, k).wait_recv()

        def drain(e, buf):
            for k in ORDER:
                gather_outer(e, buf, k).wait_send()
                gather_inner(e, buf, k).wait_send()
            for k in (0,) + ORDER:
                relay_inner(e, buf, k).wait_send()

            @pl.when(has_out)
            def _():
                for k in (0,) + ORDER:
                    relay_outer(e, buf, k).wait_send()

        def near_copy(r, k):
            ref = near_slots.at[r, near_rank]
            return cp(ref, ref, near_send.at[r], near_recv.at[r], near_peer(k))

        def far_copy(r, k):
            ref = far_slots.at[r, z]
            return cp(ref, ref, far_send.at[r], far_recv.at[r], far_peer(k))

        def near_all(r):
            ref = near_slots.at[r, pl.ds(0, near - 1)]
            return cp(ref, ref, near_send.at[r], near_recv.at[r], near_peer(1))

        def far_all(r):
            ref = far_slots.at[r, pl.ds(0, zs - 1)]
            return cp(ref, ref, far_send.at[r], far_recv.at[r], far_peer(1))

        def sum_begin(r, parts):
            parts = parts + [jnp.zeros((1, LANES), F32)] * (8 - len(parts))
            near_slots[r, near_rank] = jnp.concatenate(parts, axis=0)
            for k in range(1, near):
                near_copy(r, k).start()

        def sum_middle(r):
            near_all(r).wait_recv()
            far_slots[r, z] = jnp.sum(near_slots[r], axis=0)
            for k in range(1, zs):
                far_copy(r, k).start()

        def sum_end(r):
            far_all(r).wait_recv()
            t = jnp.sum(far_slots[r], axis=0)
            t = jnp.sum(t, axis=1, keepdims=True) * (1.0 / count)
            return jnp.broadcast_to(t, (8, LANES))

        def sum_drain(r):
            near_all(r).wait_send()
            far_all(r).wait_send()

        def row(t, i):
            return t[i : i + 1, :]

        def scalar(r):
            return r[0, 0]

        def apply(buf, done):
            def body(s, carry):
                acc = jnp.zeros((rows, cols), F32)
                for w in range(terms):
                    source = buf[s + MAXSHIFT + shifts[w]].reshape(ENV * rows, cols)
                    part = dot(left[s, w], source).astype(BF)
                    acc = acc + dot(part, right[s, w])
                return done(s, acc, carry)

            return body

        def over_sectors(body, init):
            return lax.fori_loop(0, sectors, body, init)

        def zeros(n):
            return tuple(jnp.zeros((1, LANES), F32) for _ in range(n))

        begin(0, xs_buf)
        sum_begin(0, [fold(sq)])

        def d_copies():
            piece = dall.at[own, y]
            res = [cp(piece, piece, d_send.at[0, k], d_recv.at[0, k], (sec, yy(k))) for k in range(1, ENV)]
            for k in range(ENV):
                src = dall.at[pl.ds(MAXSHIFT + in_src, 2), y]
                dst = dall.at[pl.ds(in_dst, 2), y]
                res.append(cp(src, dst, d_send.at[1, k], d_recv.at[1, k], (inner, yy(k))))
            return res

        def d_outer():
            res = []
            for k in range(ENV):
                src = dall.at[pl.ds(MAXSHIFT + out_src, 2), y]
                dst = dall.at[pl.ds(out_dst, 2), y]
                res.append(cp(src, dst, d_send.at[2, k], d_recv.at[2, k], (outer, yy(k))))
            return res

        for c in d_copies():
            c.start()

        @pl.when(has_out)
        def _():
            for c in d_outer():
                c.start()

        relay(0, xs_buf)
        sum_middle(0)
        load_left.wait()
        load_right.wait()
        for c in d_copies():
            c.wait_recv()

        @pl.when(has_out)
        def _():
            for c in d_outer():
                c.wait_recv()

        dpad[...] = jnp.ones((LANES, LANES), F32)
        for s in range(wide):
            for e in range(ENV):
                dpad[s * ENV + e : s * ENV + e + 1, 0:rows] = dall[s, e, :, 0:rows]
        dcol[...] = 1.0 / jnp.transpose(dpad[...])
        for s in range(sectors):
            rowd = jnp.zeros((1, LANES), F32)
            for e in range(ENV):
                rowd = jnp.where(y == e, dpad[(MAXSHIFT + s) * ENV + e : (MAXSHIFT + s) * ENV + e + 1, :], rowd)
            dpad[64 + s : 65 + s, :] = rowd
        mine = 1.0 / jnp.transpose(dpad[...])
        for s in range(sectors):
            dinv[s] = jnp.broadcast_to(mine[0:rows, 64 + s : 65 + s], (rows, cols))

        sum_end0 = sum_end(0)
        c0 = lax.rsqrt(row(sum_end0, 0) + 1e-06)
        c0s = scalar(c0)
        finish(0, xs_buf)

        def done0(s, acc, carry):
            a = acc * live[s] * c0s
            v = start[s] * c0s
            start[s] = v
            va[s] = a
            di = dinv[s]
            da = a * di
            vda[s] = da
            xd_buf[s + MAXSHIFT, y] = da.astype(BF)
            return (carry[0] + fold(v * a), carry[1] + fold(v * da), carry[2] + fold(v * (v * di)))

        sums = over_sectors(apply(xs_buf, done0), zeros(3))

        begin(1, xd_buf)
        sum_begin(1, list(sums))

        def scale_start(s, carry):
            for e in range(ENV):
                col = jnp.zeros((rows, 1), F32)
                col = dcol_of(s, e)
                xt_buf[s, e] = (xs_buf[s, e].astype(F32) * col * c0s).astype(BF)
            return carry

        def dcol_of(s, e):
            lane = lax.broadcasted_iota(jnp.int32, (rows, LANES), 1)
            hit = jnp.where(lane == s * ENV + e, dcol[0:rows, :], 0.0)
            return jnp.sum(hit, axis=1, keepdims=True)

        lax.fori_loop(0, wide, scale_start, 0)
        relay(1, xd_buf)
        sum_middle(1)

        def done_h(s, acc, carry):
            vh[s] = acc * live[s]
            return carry

        over_sectors(apply(xt_buf, done_h), 0)
        sum1 = sum_end(1)
        r0 = row(sum1, 0)
        along0 = row(sum1, 1) - r0 * row(sum1, 2)
        r0s, along0s = scalar(r0), scalar(along0)
        finish(1, xd_buf)

        def done1(s, acc, carry):
            a, v, di, da = va[s], start[s], dinv[s], vda[s]
            q = acc * live[s] - r0s * vh[s] - along0s * a
            corr = da - r0s * (v * di) - along0s * v
            vq[s] = q
            vc[s] = corr
            xq_buf[s + MAXSHIFT, y] = q.astype(BF)
            dq, dc = q * di, corr * di
            new = (
                corr * corr, corr * a, v * q, corr * q,
                v * dq + corr * da, corr * dq, v * dc, corr * dc,
            )
            return tuple(c + fold(n) for c, n in zip(carry, new, strict=True))

        sums = over_sectors(apply(xd_buf, done1), zeros(8))

        begin(2, xq_buf)
        sum_begin(2, list(sums))
        relay(2, xq_buf)
        sum_middle(2)
        t = sum_end(2)
        sum1_vda, sum1_vdv = row(sum1, 1), row(sum1, 2)

        def rotation(rayleigh, upper, coupling):
            px, py = upper - rayleigh, -2.0 * coupling
            big = jnp.maximum(jnp.abs(px), jnp.abs(py))
            safe = jnp.where(big > 0.0, big, 1.0)
            ux, uy = px / safe, py / safe
            h = jnp.sqrt(ux * ux + uy * uy)
            h = jnp.where(big > 0.0, h, 1.0)
            ux = jnp.where(big > 0.0, ux, 1.0)
            large = jnp.sqrt(0.5 * (1.0 + jnp.abs(ux) / h))
            small = jnp.abs(uy) / (2.0 * h * large)
            cosine = jnp.where(ux >= 0.0, large, small)
            sine = jnp.where(ux >= 0.0, small, large)
            sine = jnp.where(uy > 0.0, sine, -sine)
            half = 0.5 * (rayleigh - upper)
            ritz_value = 0.5 * (rayleigh + upper) - jnp.sqrt(half * half + coupling * coupling)
            return cosine, sine, ritz_value

        alpha = lax.rsqrt(row(t, 0) + 1e-06)
        cross = row(t, 1) + row(t, 2)
        coupling = 0.5 * alpha * cross
        upper = alpha * alpha * row(t, 3)
        cosine, sine, value0 = rotation(r0, upper, coupling)
        sa = sine * alpha
        r1 = cosine * cosine * r0 + cosine * sa * cross + sa * sa * row(t, 3)
        v_da = cosine * cosine * sum1_vda + cosine * sa * row(t, 4) + sa * sa * row(t, 5)
        v_dv = cosine * cosine * sum1_vdv + 2.0 * cosine * sa * row(t, 6) + sa * sa * row(t, 7)
        along1 = v_da - r1 * v_dv
        ritz[0:1, :] = value0
        cs, ss, r1s, l1s = scalar(cosine), scalar(sa), scalar(r1), scalar(along1)
        finish(2, xq_buf)

        def build(s, carry):
            for e in range(ENV):
                di = dcol_of(s, e)
                v = xs_buf[s, e].astype(F32) * c0s
                da = xd_buf[s, e].astype(F32)
                q = xq_buf[s, e].astype(F32)
                corr = da - v * (r0s * di + along0s)
                v1 = cs * v + ss * corr
                c1 = cs * da + ss * (q * di) - v1 * (r1s * di + l1s)
                xt_buf[s, e] = c1.astype(BF)
            return carry

        lax.fori_loop(0, wide, build, 0)

        def own_step(s, carry):
            a, v, q, corr, di = va[s], start[s], vq[s], vc[s], dinv[s]
            v1 = cs * v + ss * corr
            a1 = cs * a + ss * q
            c1 = (a1 - r1s * v1) * di - l1s * v1
            start[s] = v1
            vc[s] = c1
            return (carry[0] + fold(c1 * c1), carry[1] + fold(c1 * a1))

        pre = over_sectors(own_step, zeros(2))

        def done2(s, acc, carry):
            q = acc * live[s]
            return (carry[0] + fold(start[s] * q), carry[1] + fold(vc[s] * q))

        post = over_sectors(apply(xt_buf, done2), zeros(2))
        sum_begin(3, list(pre) + list(post))
        for e, buf in ((0, xs_buf), (1, xd_buf), (2, xq_buf)):
            drain(e, buf)
        for c in d_copies():
            c.wait_send()

        @pl.when(has_out)
        def _():
            for c in d_outer():
                c.wait_send()

        sum_middle(3)
        for r in range(3):
            sum_drain(r)
        t = sum_end(3)
        alpha = lax.rsqrt(row(t, 0) + 1e-06)
        coupling = 0.5 * alpha * (row(t, 1) + row(t, 2))
        upper = alpha * alpha * row(t, 3)
        cosine, sine, value1 = rotation(r1, upper, coupling)
        ritz[1:2, :] = value1
        cs2, ss2 = scalar(cosine), scalar(sine * alpha)
        for s in range(sectors):
            out[s] = cs2 * start[s] + ss2 * vc[s]
        sum_drain(3)

    return kernel, near, zs, wide


def local(wavefunction, left_env, right_env, shifts, block_dims, precond):
    sectors, rows, cols = wavefunction.shape
    terms = left_env.shape[1]
    nsec = lax.axis_size("sec")
    kernel, near, zs, wide = make_kernel(nsec, sectors, terms, rows, cols)
    vmem = pl.BlockSpec(memory_space=pltpu.VMEM)
    smem = pl.BlockSpec(memory_space=pltpu.SMEM)
    hbm = pl.BlockSpec(memory_space=pl.ANY)
    held = pltpu.VMEM((wide, ENV, rows, cols), BF)
    field = pltpu.VMEM((sectors, rows, cols), F32)
    dma = pltpu.SemaphoreType.DMA
    vector, ritz = pl.pallas_call(
        kernel,
        out_shape=(
            jax.ShapeDtypeStruct((sectors, rows, cols), F32),
            jax.ShapeDtypeStruct((2, LANES), F32),
        ),
        in_specs=[smem, smem, vmem, vmem, hbm, hbm],
        out_specs=(vmem, vmem),
        scratch_shapes=[
            pltpu.VMEM(left_env.shape, BF),
            pltpu.VMEM(right_env.shape, BF),
            held, held, held, held,
            pltpu.VMEM((wide, ENV, 1, LANES), F32),
            pltpu.VMEM((LANES, LANES), F32),
            pltpu.VMEM((LANES, LANES), F32),
            field, field, field, field, field, field, field, field,
            pltpu.VMEM((4, near, 8, LANES), F32),
            pltpu.VMEM((4, zs, 8, LANES), F32),
            pltpu.VMEM((8, LANES), F32),
            dma((2,)),
            dma((3, ENV)), dma((3, ENV)), dma((3, ENV)), dma((3, ENV)),
            dma((3, 4, ENV)),
            dma((3, ENV)), dma((3, ENV)),
            dma((4,)), dma((4,)), dma((4,)), dma((4,)),
        ],
        compiler_params=pltpu.CompilerParams(
            collective_id=0, has_side_effects=True, vmem_limit_bytes=48 << 20
        ),
    )(shifts, block_dims, wavefunction, precond, left_env, right_env)
    return vector, ritz[:, 0]


def solution(mesh):
    in_specs = (
        P("sec", "env", None),
        P("sec", None, "env", None),
        P("sec", None, None, None),
        P(),
        P("sec", None),
        P("sec", "env"),
    )
    out_specs = (P("sec", "env", None), P())
    return jax.shard_map(local, mesh=mesh, in_specs=in_specs, out_specs=out_specs, check_vma=False)
```

```python
import jax
import jax.numpy as jnp
from jax import lax
from jax.experimental import pallas as pl
from jax.experimental.pallas import tpu as pltpu
from jax.sharding import PartitionSpec as P

MAXSHIFT = 2
BF = jnp.bfloat16
F32 = jnp.float32
MESH = pl.DeviceIdType.MESH
ENV = 4
LANES = 128
ZS = 8
ORDER = (1, 3, 2)


def dot(a, b):
    return jnp.dot(a, b, preferred_element_type=F32)


def make_kernel(nsec, sectors, terms, rows, cols):
    zs = ZS
    xs = nsec // (2 * zs)
    near = 2 * ENV * xs
    wide = sectors + 2 * MAXSHIFT
    half = cols // 2
    count = float(nsec * sectors * ENV * rows * cols)
    halves = (0, 1)

    def kernel(
        shifts_hbm, dims_hbm, wf_hbm, prec_hbm, left_hbm, right_hbm, out, ritz,
        shifts, dims, wf, prec, left, right,
        xs0, xs1, xd0, xd1, xq0, xq1, xt0, xt1, dall, dpad, dcols, dinv,
        live, start, va, vb, vh, vq, vc, vg, tmp, near_slots, far_slots,
        load_sem, go_sem, gi_sem, out_sem, in_sem, send_sem, d_send, d_recv,
        near_send, near_recv, far_send, far_recv, ready,
    ):
        fields = ((xs0, xs1), (xd0, xd1), (xq0, xq1))
        sec = lax.axis_index("sec")
        y = lax.axis_index("env")
        core = lax.rem(sec, 2)
        chip = sec // 2
        z = lax.rem(chip, zs)
        x = chip // zs
        has_out = jnp.logical_or(
            jnp.logical_and(core == 0, sec > 0), jnp.logical_and(core == 1, sec < nsec - 1)
        )
        outer = jnp.clip(sec + 2 * core - 1, 0, nsec - 1)
        inner = sec + 1 - 2 * core
        out_src, out_dst = 2 * core, 6 * (1 - core)
        in_src, in_dst = 2 * (1 - core), 6 * core

        def yy(k):
            return lax.rem(y + k + ENV, ENV)

        near_rank = (core * ENV + y) * xs + x

        def near_peer(k):
            m = lax.rem(near_rank + k, near)
            return (((lax.rem(m, xs) * zs + z) * 2 + m // (xs * ENV)), lax.rem(m // xs, ENV))

        def far_peer(k):
            m = lax.rem(z + k + zs, zs)
            return (((x * zs + m) * 2 + core), y)

        def x_peer(k):
            return ((lax.rem(x + k, xs) * zs + z) * 2 + core, y)

        greeted = [(sec, yy(k)) for k in range(1, ENV)] + [(inner, yy(k)) for k in range(ENV)]
        greeted += [x_peer(k) for k in range(1, xs)] + [far_peer(1), far_peer(-1)]

        loads = [
            pltpu.make_async_copy(a, b, load_sem.at[i])
            for i, (a, b) in enumerate((
                (wf_hbm, wf), (dims_hbm, dims), (prec_hbm, prec), (shifts_hbm, shifts), (left_hbm, left), (right_hbm, right),
            ))
        ]
        for load in loads:
            load.start()

        zero = jnp.zeros((MAXSHIFT, ENV, rows, half), BF)
        ones = jnp.ones((MAXSHIFT, ENV, 1, LANES), F32)

        @pl.when(sec == 0)
        def _():
            for pair in fields:
                for buf in pair:
                    buf[0:MAXSHIFT] = zero
            dall[0:MAXSHIFT] = ones

        @pl.when(sec == nsec - 1)
        def _():
            for pair in fields:
                for buf in pair:
                    buf[wide - MAXSHIFT : wide] = zero
            dall[wide - MAXSHIFT : wide] = ones

        def greet(semaphore):
            for peer in greeted:
                pl.semaphore_signal(semaphore, inc=1, device_id=peer, device_id_type=MESH)

            @pl.when(has_out)
            def _():
                pl.semaphore_signal(semaphore, inc=1, device_id=(outer, y), device_id_type=MESH)

        barrier = pltpu.get_barrier_semaphore()
        greet(barrier)
        expected = len(greeted) + jnp.where(has_out, 1, 0)

        for load in loads[:3]:
            load.wait()

        def put(pair, s, value):
            for h in halves:
                pair[h][MAXSHIFT + s, y] = value[:, h * half : (h + 1) * half].astype(BF)

        def fold(v, op=jnp.add):
            parts = [
                v[r * 8 : r * 8 + 8, c * LANES : (c + 1) * LANES]
                for r in range(rows // 8)
                for c in range(cols // LANES)
            ]
            while len(parts) > 1:
                parts = [op(a, b) for a, b in zip(parts[::2], parts[1::2], strict=True)]
            return parts[0]

        row_ids = y * rows + lax.broadcasted_iota(jnp.int32, (rows, cols), 0)
        col_ids = lax.broadcasted_iota(jnp.int32, (rows, cols), 1)
        largest = jnp.zeros((8, LANES), F32)
        for s in range(sectors):
            ok = jnp.logical_and(row_ids < dims[0, s], col_ids < dims[1, s])
            mask = jnp.where(ok, 1.0, 0.0).astype(F32)
            live[s] = mask
            st = wf[s] * mask
            start[s] = st
            put(fields[0], s, st)
            largest = jnp.maximum(largest, fold(jnp.abs(st), jnp.maximum))
            dall[MAXSHIFT + s, y, :, 0:rows] = prec[s : s + 1, :]
        dpad[...] = jnp.ones((LANES, LANES), F32)
        dpad[0:sectors, 0:rows] = prec[...]
        columns = 1.0 / jnp.transpose(dpad[...])
        for s in range(sectors):
            dinv[s] = jnp.broadcast_to(columns[0:rows, s : s + 1], (rows, LANES))
        peak = jnp.max(jnp.max(largest, axis=0, keepdims=True), axis=1, keepdims=True)
        peak = jnp.broadcast_to(jnp.where(peak > 0.0, peak, 1.0), (1, LANES))

        def across(r):
            return jnp.concatenate([r] * (cols // LANES), axis=1)

        def inverse(s):
            return jnp.concatenate([dinv[s]] * (cols // LANES), axis=1)

        pl.semaphore_wait(barrier, expected)

        def cp(src, dst, ss, rs, dev):
            return pltpu.make_async_remote_copy(
                src_ref=src, dst_ref=dst, send_sem=ss, recv_sem=rs, device_id=dev, device_id_type=MESH
            )

        def gather_outer(e, h, k):
            part = fields[e][h].at[pl.ds(MAXSHIFT + out_src, 2), y]
            return cp(part, part, send_sem.at[e, h, 0, k], go_sem.at[e, h, k], (sec, yy(k)))

        def gather_inner(e, h, k):
            part = fields[e][h].at[pl.ds(MAXSHIFT + in_src, 2), y]
            return cp(part, part, send_sem.at[e, h, 1, k], gi_sem.at[e, h, k], (sec, yy(k)))

        def relay_outer(e, h, k):
            src = fields[e][h].at[pl.ds(MAXSHIFT + out_src, 2), yy(-k)]
            dst = fields[e][h].at[pl.ds(out_dst, 2), yy(-k)]
            return cp(src, dst, send_sem.at[e, h, 2, k], out_sem.at[e, h, k], (outer, y))

        def relay_inner(e, h, k):
            src = fields[e][h].at[pl.ds(MAXSHIFT + in_src, 2), yy(-k)]
            dst = fields[e][h].at[pl.ds(in_dst, 2), yy(-k)]
            return cp(src, dst, send_sem.at[e, h, 3, k], in_sem.at[e, h, k], (inner, y))

        def begin(e):
            for h in halves:
                for k in ORDER:
                    gather_outer(e, h, k).start()

            @pl.when(has_out)
            def _():
                for h in halves:
                    relay_outer(e, h, 0).start()

            for h in halves:
                for k in ORDER:
                    gather_inner(e, h, k).start()
            for h in halves:
                relay_inner(e, h, 0).start()

        def pass_outer(e):
            for h in halves:
                for k in ORDER:
                    gather_outer(e, h, k).wait_recv()

                    @pl.when(has_out)
                    def _():
                        relay_outer(e, h, k).start()

        def pass_inner(e):
            for h in halves:
                for k in ORDER:
                    gather_inner(e, h, k).wait_recv()
                    relay_inner(e, h, k).start()

        def finish(e, h):
            @pl.when(has_out)
            def _():
                for k in (0,) + ORDER:
                    relay_outer(e, h, k).wait_recv()

            for k in (0,) + ORDER:
                relay_inner(e, h, k).wait_recv()

        def drain(e):
            for h in halves:
                for k in ORDER:
                    gather_outer(e, h, k).wait_send()
                    gather_inner(e, h, k).wait_send()
                for k in (0,) + ORDER:
                    relay_inner(e, h, k).wait_send()

                @pl.when(has_out)
                def _():
                    for k in (0,) + ORDER:
                        relay_outer(e, h, k).wait_send()

        def near_copy(r, k):
            ref = near_slots.at[r, near_rank]
            return cp(ref, ref, near_send.at[r], near_recv.at[r], near_peer(k))

        def far_copy(r, k):
            ref = far_slots.at[r, z]
            return cp(ref, ref, far_send.at[r], far_recv.at[r], far_peer(k))

        def near_all(r):
            ref = near_slots.at[r, pl.ds(0, near - 1)]
            return cp(ref, ref, near_send.at[r], near_recv.at[r], near_peer(1))

        def far_all(r):
            ref = far_slots.at[r, pl.ds(0, zs - 1)]
            return cp(ref, ref, far_send.at[r], far_recv.at[r], far_peer(1))

        def sum_begin(r, parts, last=None):
            parts = [jnp.sum(p, axis=0, keepdims=True) for p in parts]
            parts = parts + [jnp.zeros((1, LANES), F32)] * (8 - len(parts))
            if last is not None:
                parts[7] = last
            near_slots[r, near_rank] = jnp.concatenate(parts, axis=0)
            for k in range(1, near):
                near_copy(r, k).start()

        def total_of(slots, scaled):
            t = slots
            if not scaled:
                return jnp.sum(t, axis=0)
            scale = t[:, 7:8, :]
            top = jnp.max(scale, axis=0, keepdims=True)
            ratio = scale / top
            t = jnp.sum(t * (ratio * ratio), axis=0)
            keep = lax.broadcasted_iota(jnp.int32, (8, LANES), 0) == 7
            return jnp.where(keep, jnp.broadcast_to(top[0], (8, LANES)), t)

        def sum_middle(r, scaled=False):
            near_all(r).wait_recv()
            far_slots[r, z] = total_of(near_slots[r], scaled)
            for k in range(1, zs):
                far_copy(r, k).start()

        def sum_end(r, scaled=False):
            far_all(r).wait_recv()
            t = total_of(far_slots[r], scaled)
            m = jnp.sum(t, axis=1, keepdims=True) * (1.0 / count)
            return jnp.broadcast_to(m, (8, LANES)), t[7:8, :]

        def sum_drain(r):
            near_all(r).wait_send()
            far_all(r).wait_send()

        def row(t, i):
            return t[i : i + 1, :]

        def h_half(pair, h, s):
            acc = jnp.zeros((rows, cols), F32)
            for w in range(terms):
                source = pair[h][s + MAXSHIFT + shifts[w]].reshape(ENV * rows, half)
                part = dot(left[s, w], source).astype(BF)
                acc = acc + dot(part, right[s, w, h * half : (h + 1) * half, :])
            return acc

        def apply_arriving(e, done):
            finish(e, 0)
            for s in range(sectors):
                tmp[s] = h_half(fields[e], 0, s)
            finish(e, 1)
            for s in range(sectors):
                done(s, (tmp[s] + h_half(fields[e], 1, s)) * live[s])

        def apply_built(dst):
            for s in range(sectors):
                dst[s] = h_half((xt0, xt1), 0, s)
            for s in range(sectors):
                dst[s] = (dst[s] + h_half((xt0, xt1), 1, s)) * live[s]

        begin(0)
        greet(ready.at[0])

        def d_copies():
            piece = dall.at[pl.ds(MAXSHIFT, sectors), y]
            res = [cp(piece, piece, d_send.at[0, k], d_recv.at[0, k], (sec, yy(k))) for k in range(1, ENV)]
            for k in range(ENV):
                src = dall.at[pl.ds(MAXSHIFT + in_src, 2), y]
                dst = dall.at[pl.ds(in_dst, 2), y]
                res.append(cp(src, dst, d_send.at[1, k], d_recv.at[1, k], (inner, yy(k))))
            return res

        def d_outer():
            res = []
            for k in range(ENV):
                src = dall.at[pl.ds(MAXSHIFT + out_src, 2), y]
                dst = dall.at[pl.ds(out_dst, 2), y]
                res.append(cp(src, dst, d_send.at[2, k], d_recv.at[2, k], (outer, yy(k))))
            return res

        for c in d_copies():
            c.start()
        pl.semaphore_wait(ready.at[0], expected)
        for k in (2, -2):
            pl.semaphore_signal(ready.at[1], inc=1, device_id=far_peer(k), device_id_type=MESH)

        @pl.when(has_out)
        def _():
            for c in d_outer():
                c.start()

        pass_outer(0)
        pass_inner(0)
        for load in loads[3:]:
            load.wait()
        inv_peak = across(1.0 / peak)
        sums = [jnp.zeros((8, LANES), F32) for _ in range(4)]

        def done0(s, a):
            di = inverse(s)
            da = a * di
            va[s] = a
            put(fields[1], s, da)
            u = start[s] * inv_peak
            ua = a * inv_peak
            for i, n in enumerate((u * u, u * ua, u * (ua * di), u * (u * di))):
                sums[i] = sums[i] + fold(n)

        apply_arriving(0, done0)

        pl.semaphore_wait(ready.at[1], 2)
        sum_begin(1, sums, peak)
        begin(1)
        for c in d_copies():
            c.wait_recv()

        @pl.when(has_out)
        def _():
            for c in d_outer():
                c.wait_recv()

        for s in range(wide):
            for e in range(ENV):
                dpad[s * ENV + e : s * ENV + e + 1, 0:rows] = dall[s, e, :, 0:rows]
        columns = 1.0 / jnp.transpose(dpad[...])
        for s in range(wide):
            for e in range(ENV):
                k = s * ENV + e
                dcols[s, e] = jnp.broadcast_to(columns[0:rows, k : k + 1], (rows, LANES))

        def scale_start(s, carry):
            for h in halves:
                for e in range(ENV):
                    (xt0, xt1)[h][s, e] = (fields[0][h][s, e].astype(F32) * dcols[s, e]).astype(BF)
            return carry

        lax.fori_loop(0, wide, scale_start, 0)
        apply_built(vh)
        pass_outer(1)
        sum_middle(1, True)
        pass_inner(1)

        def done1(s, b):
            vb[s] = b

        apply_arriving(1, done1)
        t, top = sum_end(1, True)
        c0 = lax.rsqrt(top * (top * row(t, 0)) + 1e-06)
        k2 = (c0 * top) * (c0 * top)
        r0, v_da0, v_dv0 = k2 * row(t, 1), k2 * row(t, 2), k2 * row(t, 3)
        along0 = v_da0 - r0 * v_dv0
        c0w, r0w, l0w = across(c0), across(r0), across(along0)
        sums = [jnp.zeros((8, LANES), F32) for _ in range(8)]
        for s in range(sectors):
            di = inverse(s)
            v, a, hd, b = start[s] * c0w, va[s] * c0w, vh[s] * c0w, vb[s] * c0w
            da = a * di
            q = b - r0w * hd - l0w * a
            corr = da - r0w * (v * di) - l0w * v
            dq, dc = q * di, corr * di
            put(fields[2], s, dq)
            start[s], va[s], vh[s], vb[s], vq[s], vc[s] = v, a, hd, b, q, corr
            new = (
                corr * corr, corr * a, v * q, corr * q,
                v * dq + corr * da, corr * dq, v * dc, corr * dc,
            )
            sums = [c + fold(n) for c, n in zip(sums, new, strict=True)]

        sum_begin(2, sums)
        begin(2)

        def build(s, carry):
            for e in range(ENV):
                di = dcols[s, e]
                for_da = c0 * di
                for_s = -for_da * (r0 * di + along0)
                for h in halves:
                    da = fields[1][h][s, e].astype(F32)
                    st = fields[0][h][s, e].astype(F32)
                    (xt0, xt1)[h][s, e] = (for_da * da + for_s * st).astype(BF)
            return carry

        lax.fori_loop(0, wide, build, 0)
        apply_built(vg)
        pass_outer(2)
        sum_middle(2)
        pass_inner(2)

        def done2(s, n):
            tmp[s] = n

        apply_arriving(2, done2)
        t, _ = sum_end(2)

        def rotation(rayleigh, upper, coupling):
            px, py = upper - rayleigh, -2.0 * coupling
            big = jnp.maximum(jnp.abs(px), jnp.abs(py))
            some = big > 0.0
            safe = jnp.where(some, big, 1.0)
            ux, uy = jnp.where(some, px / safe, 1.0), py / safe
            h = jnp.sqrt(ux * ux + uy * uy)
            large = jnp.sqrt(0.5 * (1.0 + jnp.abs(ux) / h))
            small = jnp.abs(uy) / (2.0 * h * large)
            cosine = jnp.where(ux >= 0.0, large, small)
            sine = jnp.where(ux >= 0.0, small, large)
            sine = jnp.where(uy > 0.0, sine, -sine)
            mid = 0.5 * (rayleigh - upper)
            return cosine, sine, 0.5 * (rayleigh + upper) - jnp.sqrt(mid * mid + coupling * coupling)

        alpha = lax.rsqrt(row(t, 0) + 1e-06)
        cross = row(t, 1) + row(t, 2)
        cosine, sine, value0 = rotation(r0, alpha * alpha * row(t, 3), 0.5 * alpha * cross)
        sa = sine * alpha
        r1 = cosine * cosine * r0 + cosine * sa * cross + sa * sa * row(t, 3)
        v_da = cosine * cosine * v_da0 + cosine * sa * row(t, 4) + sa * sa * row(t, 5)
        v_dv = cosine * cosine * v_dv0 + 2.0 * cosine * sa * row(t, 6) + sa * sa * row(t, 7)
        along1 = v_da - r1 * v_dv
        ritz[0:1, :] = value0
        cw, sw, r1w, l1w = across(cosine), across(sa), across(r1), across(along1)
        sums = [jnp.zeros((8, LANES), F32) for _ in range(4)]
        for s in range(sectors):
            di = inverse(s)
            v1 = cw * start[s] + sw * vc[s]
            a1 = cw * va[s] + sw * vq[s]
            c1 = (a1 - r1w * v1) * di - l1w * v1
            q1 = cw * vb[s] + sw * tmp[s] - r1w * (cw * vh[s] + sw * vg[s]) - l1w * a1
            start[s] = v1
            vc[s] = c1
            sums = [c + fold(n) for c, n in zip(sums, (c1 * c1, c1 * a1, v1 * q1, c1 * q1), strict=True)]
        sum_begin(0, sums)
        for e in range(3):
            drain(e)
        for c in d_copies():
            c.wait_send()

        @pl.when(has_out)
        def _():
            for c in d_outer():
                c.wait_send()

        sum_middle(0)
        for r in (1, 2):
            sum_drain(r)
        t, _ = sum_end(0)
        alpha = lax.rsqrt(row(t, 0) + 1e-06)
        coupling = 0.5 * alpha * (row(t, 1) + row(t, 2))
        cosine, sine, value1 = rotation(r1, alpha * alpha * row(t, 3), coupling)
        ritz[1:2, :] = value1
        cw, sw = across(cosine), across(sine * alpha)
        for s in range(sectors):
            out[s] = cw * start[s] + sw * vc[s]
        sum_drain(0)

    return kernel, near, zs, wide, half


def local(wavefunction, left_env, right_env, shifts, block_dims, precond):
    sectors, rows, cols = wavefunction.shape
    terms = left_env.shape[1]
    nsec = lax.axis_size("sec")
    kernel, near, zs, wide, half = make_kernel(nsec, sectors, terms, rows, cols)
    vmem = pl.BlockSpec(memory_space=pltpu.VMEM)
    hbm = pl.BlockSpec(memory_space=pltpu.HBM)
    held = pltpu.VMEM((wide, ENV, rows, half), BF)
    field = pltpu.VMEM((sectors, rows, cols), F32)
    dma = pltpu.SemaphoreType.DMA
    vector, ritz = pl.pallas_call(
        kernel,
        out_shape=(
            jax.ShapeDtypeStruct((sectors, rows, cols), F32),
            jax.ShapeDtypeStruct((2, LANES), F32),
        ),
        in_specs=[hbm] * 6,
        out_specs=(vmem, vmem),
        scratch_shapes=[
            pltpu.SMEM(shifts.shape, jnp.int32),
            pltpu.SMEM((2, sectors), jnp.int32),
            pltpu.VMEM(wavefunction.shape, F32),
            pltpu.VMEM(precond.shape, F32),
            pltpu.VMEM(left_env.shape, BF),
            pltpu.VMEM(right_env.shape, BF),
            held, held, held, held, held, held, held, held,
            pltpu.VMEM((wide, ENV, 1, LANES), F32),
            pltpu.VMEM((LANES, LANES), F32),
            pltpu.VMEM((wide, ENV, rows, LANES), F32),
            pltpu.VMEM((sectors, rows, LANES), F32),
            field, field, field, field, field, field, field, field, field,
            pltpu.VMEM((3, near, 8, LANES), F32),
            pltpu.VMEM((3, zs, 8, LANES), F32),
            dma((6,)),
            dma((3, 2, ENV)), dma((3, 2, ENV)), dma((3, 2, ENV)), dma((3, 2, ENV)),
            dma((3, 2, 4, ENV)),
            dma((3, ENV)), dma((3, ENV)),
            dma((3,)), dma((3,)), dma((3,)), dma((3,)),
            pltpu.SemaphoreType.REGULAR((2,)),
        ],
        compiler_params=pltpu.CompilerParams(
            collective_id=0, has_side_effects=True, vmem_limit_bytes=56 << 20
        ),
    )(shifts, block_dims.T, wavefunction, precond, left_env, right_env)
    return vector, ritz[:, 0]


def solution(mesh):
    in_specs = (
        P("sec", "env", None),
        P("sec", None, "env", None),
        P("sec", None, None, None),
        P(),
        P("sec", None),
        P("sec", "env"),
    )
    out_specs = (P("sec", "env", None), P())
    return jax.shard_map(local, mesh=mesh, in_specs=in_specs, out_specs=out_specs, check_vma=False)
```

```python
import jax
import jax.numpy as jnp
from jax import lax
from jax.experimental import pallas as pl
from jax.experimental.pallas import tpu as pltpu
from jax.sharding import PartitionSpec as P

MAXSHIFT = 2
BF = jnp.bfloat16
F32 = jnp.float32
MESH = pl.DeviceIdType.MESH
ENV = 4
LANES = 128
ZS = 8
ORDER = (1, 3, 2)


def dot(a, b):
    return jnp.dot(a, b, preferred_element_type=F32)


def make_kernel(nsec, sectors, terms, rows, cols):
    zs = ZS
    xs = nsec // (2 * zs)
    near = 2 * ENV * xs
    wide = sectors + 2 * MAXSHIFT
    half = cols // 2
    count = float(nsec * sectors * ENV * rows * cols)
    halves = (0, 1)

    def kernel(
        shifts_hbm, dims_hbm, wf_hbm, prec_hbm, left_hbm, right_hbm, out, ritz,
        shifts, dims, wf, prec, left, right,
        xs0, xs1, xd0, xd1, xq0, xq1, xt0, xt1, dall, dpad, dcols, dinv,
        live, start, va, vb, vh, vq, vc, vg, tmp, near_slots, far_slots,
        load_sem, go_sem, gi_sem, out_sem, in_sem, send_sem, d_send, d_recv,
        near_send, near_recv, far_send, far_recv, ready,
    ):
        fields = ((xs0, xs1), (xd0, xd1), (xq0, xq1))
        sec = lax.axis_index("sec")
        y = lax.axis_index("env")
        core = lax.rem(sec, 2)
        chip = sec // 2
        z = lax.rem(chip, zs)
        x = chip // zs
        has_out = jnp.logical_or(
            jnp.logical_and(core == 0, sec > 0), jnp.logical_and(core == 1, sec < nsec - 1)
        )
        outer = jnp.clip(sec + 2 * core - 1, 0, nsec - 1)
        inner = sec + 1 - 2 * core
        out_src, out_dst = 2 * core, 6 * (1 - core)
        in_src, in_dst = 2 * (1 - core), 6 * core

        def yy(k):
            return lax.rem(y + k + ENV, ENV)

        near_rank = (core * ENV + y) * xs + x

        def near_peer(k):
            m = lax.rem(near_rank + k, near)
            return (((lax.rem(m, xs) * zs + z) * 2 + m // (xs * ENV)), lax.rem(m // xs, ENV))

        def far_peer(k):
            m = lax.rem(z + k + zs, zs)
            return (((x * zs + m) * 2 + core), y)

        def x_peer(k):
            return ((lax.rem(x + k, xs) * zs + z) * 2 + core, y)

        greeted = [(sec, yy(k)) for k in range(1, ENV)] + [(inner, yy(k)) for k in range(ENV)]
        greeted += [x_peer(k) for k in range(1, xs)] + [far_peer(1), far_peer(-1)]

        loads = [
            pltpu.make_async_copy(a, b, load_sem.at[i])
            for i, (a, b) in enumerate((
                (wf_hbm, wf), (dims_hbm, dims), (prec_hbm, prec), (shifts_hbm, shifts), (left_hbm, left), (right_hbm, right),
            ))
        ]
        for load in loads:
            load.start()

        zero = jnp.zeros((MAXSHIFT, ENV, rows, half), BF)
        ones = jnp.ones((MAXSHIFT, ENV, 1, LANES), F32)

        @pl.when(sec == 0)
        def _():
            for pair in fields:
                for buf in pair:
                    buf[0:MAXSHIFT] = zero
            dall[0:MAXSHIFT] = ones

        @pl.when(sec == nsec - 1)
        def _():
            for pair in fields:
                for buf in pair:
                    buf[wide - MAXSHIFT : wide] = zero
            dall[wide - MAXSHIFT : wide] = ones

        def greet(semaphore):
            for peer in greeted:
                pl.semaphore_signal(semaphore, inc=1, device_id=peer, device_id_type=MESH)

            @pl.when(has_out)
            def _():
                pl.semaphore_signal(semaphore, inc=1, device_id=(outer, y), device_id_type=MESH)

        barrier = pltpu.get_barrier_semaphore()
        greet(barrier)
        expected = len(greeted) + jnp.where(has_out, 1, 0)

        for load in loads[:3]:
            load.wait()

        def put(pair, s, value):
            for h in halves:
                pair[h][MAXSHIFT + s, y] = value[:, h * half : (h + 1) * half].astype(BF)

        def fold(v, op=jnp.add):
            parts = [
                v[r * 8 : r * 8 + 8, c * LANES : (c + 1) * LANES]
                for r in range(rows // 8)
                for c in range(cols // LANES)
            ]
            while len(parts) > 1:
                parts = [op(a, b) for a, b in zip(parts[::2], parts[1::2], strict=True)]
            return parts[0]

        row_ids = y * rows + lax.broadcasted_iota(jnp.int32, (rows, cols), 0)
        col_ids = lax.broadcasted_iota(jnp.int32, (rows, cols), 1)
        largest = jnp.zeros((8, LANES), F32)
        for s in range(sectors):
            ok = jnp.logical_and(row_ids < dims[0, s], col_ids < dims[1, s])
            mask = jnp.where(ok, 1.0, 0.0).astype(F32)
            live[s] = mask
            st = wf[s] * mask
            start[s] = st
            put(fields[0], s, st)
            largest = jnp.maximum(largest, fold(jnp.abs(st), jnp.maximum))
            dall[MAXSHIFT + s, y, :, 0:rows] = prec[s : s + 1, :]
        dpad[...] = jnp.ones((LANES, LANES), F32)
        dpad[0:sectors, 0:rows] = prec[...]
        columns = 1.0 / jnp.transpose(dpad[...])
        for s in range(sectors):
            dinv[s] = jnp.broadcast_to(columns[0:rows, s : s + 1], (rows, LANES))
        peak = jnp.max(jnp.max(largest, axis=0, keepdims=True), axis=1, keepdims=True)
        peak = jnp.broadcast_to(jnp.where(peak > 0.0, peak, 1.0), (1, LANES))

        def across(r):
            return jnp.concatenate([r] * (cols // LANES), axis=1)

        def inverse(s):
            return jnp.concatenate([dinv[s]] * (cols // LANES), axis=1)

        pl.semaphore_wait(barrier, expected)

        def cp(src, dst, ss, rs, dev):
            return pltpu.make_async_remote_copy(
                src_ref=src, dst_ref=dst, send_sem=ss, recv_sem=rs, device_id=dev, device_id_type=MESH
            )

        def gather_outer(e, h, k):
            part = fields[e][h].at[pl.ds(MAXSHIFT + out_src, 2), y]
            return cp(part, part, send_sem.at[e, h, 0, k], go_sem.at[e, h, k], (sec, yy(k)))

        def gather_inner(e, h, k):
            part = fields[e][h].at[pl.ds(MAXSHIFT + in_src, 2), y]
            return cp(part, part, send_sem.at[e, h, 1, k], gi_sem.at[e, h, k], (sec, yy(k)))

        def relay_outer(e, h, k):
            src = fields[e][h].at[pl.ds(MAXSHIFT + out_src, 2), yy(-k)]
            dst = fields[e][h].at[pl.ds(out_dst, 2), yy(-k)]
            return cp(src, dst, send_sem.at[e, h, 2, k], out_sem.at[e, h, k], (outer, y))

        def relay_inner(e, h, k):
            src = fields[e][h].at[pl.ds(MAXSHIFT + in_src, 2), yy(-k)]
            dst = fields[e][h].at[pl.ds(in_dst, 2), yy(-k)]
            return cp(src, dst, send_sem.at[e, h, 3, k], in_sem.at[e, h, k], (inner, y))

        def begin(e):
            for h in halves:
                for k in ORDER:
                    gather_outer(e, h, k).start()

            @pl.when(has_out)
            def _():
                for h in halves:
                    relay_outer(e, h, 0).start()

            for h in halves:
                for k in ORDER:
                    gather_inner(e, h, k).start()
            for h in halves:
                relay_inner(e, h, 0).start()

        def pass_outer(e):
            for h in halves:
                for k in ORDER:
                    gather_outer(e, h, k).wait_recv()

                    @pl.when(has_out)
                    def _():
                        relay_outer(e, h, k).start()

        def pass_inner(e):
            for h in halves:
                for k in ORDER:
                    gather_inner(e, h, k).wait_recv()
                    relay_inner(e, h, k).start()

        def finish(e, h):
            @pl.when(has_out)
            def _():
                for k in (0,) + ORDER:
                    relay_outer(e, h, k).wait_recv()

            for k in (0,) + ORDER:
                relay_inner(e, h, k).wait_recv()

        def drain(e):
            for h in halves:
                for k in ORDER:
                    gather_outer(e, h, k).wait_send()
                    gather_inner(e, h, k).wait_send()
                for k in (0,) + ORDER:
                    relay_inner(e, h, k).wait_send()

                @pl.when(has_out)
                def _():
                    for k in (0,) + ORDER:
                        relay_outer(e, h, k).wait_send()

        def near_copy(r, k):
            ref = near_slots.at[r, near_rank]
            return cp(ref, ref, near_send.at[r], near_recv.at[r], near_peer(k))

        def far_copy(r, k):
            ref = far_slots.at[r, z]
            return cp(ref, ref, far_send.at[r], far_recv.at[r], far_peer(k))

        def near_all(r):
            ref = near_slots.at[r, pl.ds(0, near - 1)]
            return cp(ref, ref, near_send.at[r], near_recv.at[r], near_peer(1))

        def far_all(r):
            ref = far_slots.at[r, pl.ds(0, zs - 1)]
            return cp(ref, ref, far_send.at[r], far_recv.at[r], far_peer(1))

        def sum_begin(r, parts, last=None):
            parts = [jnp.sum(p, axis=0, keepdims=True) for p in parts]
            parts = parts + [jnp.zeros((1, LANES), F32)] * (8 - len(parts))
            if last is not None:
                parts[7] = last
            near_slots[r, near_rank] = jnp.concatenate(parts, axis=0)
            for k in range(1, near):
                near_copy(r, k).start()

        def total_of(slots, scaled):
            t = slots
            if not scaled:
                return jnp.sum(t, axis=0)
            scale = t[:, 7:8, :]
            top = jnp.max(scale, axis=0, keepdims=True)
            ratio = scale / top
            t = jnp.sum(t * (ratio * ratio), axis=0)
            keep = lax.broadcasted_iota(jnp.int32, (8, LANES), 0) == 7
            return jnp.where(keep, jnp.broadcast_to(top[0], (8, LANES)), t)

        def sum_middle(r, scaled=False):
            near_all(r).wait_recv()
            far_slots[r, z] = total_of(near_slots[r], scaled)
            for k in range(1, zs):
                far_copy(r, k).start()

        def sum_end(r, scaled=False):
            far_all(r).wait_recv()
            t = total_of(far_slots[r], scaled)
            m = jnp.sum(t, axis=1, keepdims=True) * (1.0 / count)
            return jnp.broadcast_to(m, (8, LANES)), t[7:8, :]

        def sum_drain(r):
            near_all(r).wait_send()
            far_all(r).wait_send()

        def row(t, i):
            return t[i : i + 1, :]

        def h_half(pair, h, s):
            acc = jnp.zeros((rows, cols), F32)
            for w in range(terms):
                source = pair[h][s + MAXSHIFT + shifts[w]].reshape(ENV * rows, half)
                part = dot(left[s, w], source).astype(BF)
                acc = acc + dot(part, right[s, w, h * half : (h + 1) * half, :])
            return acc

        def apply_arriving(e, done):
            finish(e, 0)
            for s in range(sectors):
                tmp[s] = h_half(fields[e], 0, s)
            finish(e, 1)
            for s in range(sectors):
                done(s, (tmp[s] + h_half(fields[e], 1, s)) * live[s])

        def apply_built(dst):
            for s in range(sectors):
                dst[s] = h_half((xt0, xt1), 0, s)
            for s in range(sectors):
                dst[s] = (dst[s] + h_half((xt0, xt1), 1, s)) * live[s]

        begin(0)
        greet(ready.at[0])

        def d_copies():
            piece = dall.at[pl.ds(MAXSHIFT, sectors), y]
            res = [cp(piece, piece, d_send.at[0, k], d_recv.at[0, k], (sec, yy(k))) for k in range(1, ENV)]
            for k in range(ENV):
                src = dall.at[pl.ds(MAXSHIFT + in_src, 2), y]
                dst = dall.at[pl.ds(in_dst, 2), y]
                res.append(cp(src, dst, d_send.at[1, k], d_recv.at[1, k], (inner, yy(k))))
            return res

        def d_outer():
            res = []
            for k in range(ENV):
                src = dall.at[pl.ds(MAXSHIFT + out_src, 2), y]
                dst = dall.at[pl.ds(out_dst, 2), y]
                res.append(cp(src, dst, d_send.at[2, k], d_recv.at[2, k], (outer, yy(k))))
            return res

        for c in d_copies():
            c.start()
        pl.semaphore_wait(ready.at[0], expected)
        for k in (2, -2):
            pl.semaphore_signal(ready.at[1], inc=1, device_id=far_peer(k), device_id_type=MESH)

        @pl.when(has_out)
        def _():
            for c in d_outer():
                c.start()

        pass_outer(0)
        pass_inner(0)
        for load in loads[3:]:
            load.wait()
        inv_peak = across(1.0 / peak)
        sums = [jnp.zeros((8, LANES), F32) for _ in range(4)]

        def done0(s, a):
            di = inverse(s)
            da = a * di
            va[s] = a
            put(fields[1], s, da)
            u = start[s] * inv_peak
            ua = a * inv_peak
            for i, n in enumerate((u * u, u * ua, u * (ua * di), u * (u * di))):
                sums[i] = sums[i] + fold(n)

        apply_arriving(0, done0)

        pl.semaphore_wait(ready.at[1], 2)
        sum_begin(1, sums, peak)
        begin(1)
        for c in d_copies():
            c.wait_recv()

        @pl.when(has_out)
        def _():
            for c in d_outer():
                c.wait_recv()

        for s in range(wide):
            for e in range(ENV):
                dpad[s * ENV + e : s * ENV + e + 1, 0:rows] = dall[s, e, :, 0:rows]
        columns = 1.0 / jnp.transpose(dpad[...])
        for s in range(wide):
            for e in range(ENV):
                k = s * ENV + e
                dcols[s, e] = jnp.broadcast_to(columns[0:rows, k : k + 1], (rows, LANES))

        def scale_start(s, carry):
            for h in halves:
                for e in range(ENV):
                    (xt0, xt1)[h][s, e] = (fields[0][h][s, e].astype(F32) * dcols[s, e]).astype(BF)
            return carry

        lax.fori_loop(0, wide, scale_start, 0)
        apply_built(vh)
        pass_outer(1)
        sum_middle(1, True)
        pass_inner(1)

        def done1(s, b):
            vb[s] = b

        apply_arriving(1, done1)
        t, top = sum_end(1, True)
        c0 = lax.rsqrt(top * (top * row(t, 0)) + 1e-06)
        k2 = (c0 * top) * (c0 * top)
        r0, v_da0, v_dv0 = k2 * row(t, 1), k2 * row(t, 2), k2 * row(t, 3)
        along0 = v_da0 - r0 * v_dv0
        c0w, r0w, l0w = across(c0), across(r0), across(along0)
        sums = [jnp.zeros((8, LANES), F32) for _ in range(8)]
        for s in range(sectors):
            di = inverse(s)
            v, a, hd, b = start[s] * c0w, va[s] * c0w, vh[s] * c0w, vb[s] * c0w
            da = a * di
            q = b - r0w * hd - l0w * a
            corr = da - r0w * (v * di) - l0w * v
            dq, dc = q * di, corr * di
            put(fields[2], s, dq)
            start[s], va[s], vh[s], vb[s], vq[s], vc[s] = v, a, hd, b, q, corr
            new = (
                corr * corr, corr * a, v * q, corr * q,
                v * dq + corr * da, corr * dq, v * dc, corr * dc,
            )
            sums = [c + fold(n) for c, n in zip(sums, new, strict=True)]

        sum_begin(2, sums)
        begin(2)

        def build(s, carry):
            for e in range(ENV):
                di = dcols[s, e]
                for_da = c0 * di
                for_s = -for_da * (r0 * di + along0)
                for h in halves:
                    da = fields[1][h][s, e].astype(F32)
                    st = fields[0][h][s, e].astype(F32)
                    (xt0, xt1)[h][s, e] = (for_da * da + for_s * st).astype(BF)
            return carry

        lax.fori_loop(0, wide, build, 0)
        apply_built(vg)
        pass_outer(2)
        sum_middle(2)
        pass_inner(2)

        def done2(s, n):
            tmp[s] = n

        apply_arriving(2, done2)
        t, _ = sum_end(2)

        def rotation(rayleigh, upper, coupling):
            px, py = upper - rayleigh, -2.0 * coupling
            big = jnp.maximum(jnp.abs(px), jnp.abs(py))
            some = big > 0.0
            safe = jnp.where(some, big, 1.0)
            ux, uy = jnp.where(some, px / safe, 1.0), py / safe
            h = jnp.sqrt(ux * ux + uy * uy)
            large = jnp.sqrt(0.5 * (1.0 + jnp.abs(ux) / h))
            small = jnp.abs(uy) / (2.0 * h * large)
            cosine = jnp.where(ux >= 0.0, large, small)
            sine = jnp.where(ux >= 0.0, small, large)
            sine = jnp.where(uy > 0.0, sine, -sine)
            mid = 0.5 * (rayleigh - upper)
            return cosine, sine, 0.5 * (rayleigh + upper) - jnp.sqrt(mid * mid + coupling * coupling)

        alpha = lax.rsqrt(row(t, 0) + 1e-06)
        cross = row(t, 1) + row(t, 2)
        cosine, sine, value0 = rotation(r0, alpha * alpha * row(t, 3), 0.5 * alpha * cross)
        sa = sine * alpha
        r1 = cosine * cosine * r0 + cosine * sa * cross + sa * sa * row(t, 3)
        v_da = cosine * cosine * v_da0 + cosine * sa * row(t, 4) + sa * sa * row(t, 5)
        v_dv = cosine * cosine * v_dv0 + 2.0 * cosine * sa * row(t, 6) + sa * sa * row(t, 7)
        along1 = v_da - r1 * v_dv
        ritz[0:1, :] = value0
        cw, sw, r1w, l1w = across(cosine), across(sa), across(r1), across(along1)
        sums = [jnp.zeros((8, LANES), F32) for _ in range(4)]
        for s in range(sectors):
            di = inverse(s)
            v1 = cw * start[s] + sw * vc[s]
            a1 = cw * va[s] + sw * vq[s]
            c1 = (a1 - r1w * v1) * di - l1w * v1
            q1 = cw * vb[s] + sw * tmp[s] - r1w * (cw * vh[s] + sw * vg[s]) - l1w * a1
            start[s] = v1
            vc[s] = c1
            sums = [c + fold(n) for c, n in zip(sums, (c1 * c1, c1 * a1, v1 * q1, c1 * q1), strict=True)]
        sum_begin(0, sums)
        for e in range(3):
            drain(e)
        for c in d_copies():
            c.wait_send()

        @pl.when(has_out)
        def _():
            for c in d_outer():
                c.wait_send()

        sum_middle(0)
        for r in (1, 2):
            sum_drain(r)
        t, _ = sum_end(0)
        alpha = lax.rsqrt(row(t, 0) + 1e-06)
        coupling = 0.5 * alpha * (row(t, 1) + row(t, 2))
        cosine, sine, value1 = rotation(r1, alpha * alpha * row(t, 3), coupling)
        ritz[1:2, :] = value1
        cw, sw = across(cosine), across(sine * alpha)
        for s in range(sectors):
            out[s] = cw * start[s] + sw * vc[s]
        sum_drain(0)

    return kernel, near, zs, wide, half


def local(wavefunction, left_env, right_env, shifts, block_dims, precond):
    sectors, rows, cols = wavefunction.shape
    terms = left_env.shape[1]
    nsec = lax.axis_size("sec")
    kernel, near, zs, wide, half = make_kernel(nsec, sectors, terms, rows, cols)
    vmem = pl.BlockSpec(memory_space=pltpu.VMEM)
    hbm = pl.BlockSpec(memory_space=pltpu.HBM)
    held = pltpu.VMEM((wide, ENV, rows, half), BF)
    field = pltpu.VMEM((sectors, rows, cols), F32)
    dma = pltpu.SemaphoreType.DMA
    vector, ritz = pl.pallas_call(
        kernel,
        out_shape=(
            jax.ShapeDtypeStruct((sectors, rows, cols), F32),
            jax.ShapeDtypeStruct((2, LANES), F32),
        ),
        in_specs=[hbm] * 6,
        out_specs=(vmem, vmem),
        scratch_shapes=[
            pltpu.SMEM(shifts.shape, jnp.int32),
            pltpu.SMEM((2, sectors), jnp.int32),
            pltpu.VMEM(wavefunction.shape, F32),
            pltpu.VMEM(precond.shape, F32),
            pltpu.VMEM(left_env.shape, BF),
            pltpu.VMEM(right_env.shape, BF),
            held, held, held, held, held, held, held, held,
            pltpu.VMEM((wide, ENV, 1, LANES), F32),
            pltpu.VMEM((LANES, LANES), F32),
            pltpu.VMEM((wide, ENV, rows, LANES), F32),
            pltpu.VMEM((sectors, rows, LANES), F32),
            field, field, field, field, field, field, field, field, field,
            pltpu.VMEM((3, near, 8, LANES), F32),
            pltpu.VMEM((3, zs, 8, LANES), F32),
            dma((6,)),
            dma((3, 2, ENV)), dma((3, 2, ENV)), dma((3, 2, ENV)), dma((3, 2, ENV)),
            dma((3, 2, 4, ENV)),
            dma((3, ENV)), dma((3, ENV)),
            dma((3,)), dma((3,)), dma((3,)), dma((3,)),
            pltpu.SemaphoreType.REGULAR((2,)),
        ],
        compiler_params=pltpu.CompilerParams(
            collective_id=0, has_side_effects=True, vmem_limit_bytes=40 << 20
        ),
    )(*(pltpu.with_memory_space_constraint(a, pltpu.HBM) for a in (shifts, block_dims.T, wavefunction, precond, left_env, right_env)))
    return vector, ritz[:, 0]


def solution(mesh):
    in_specs = (
        P("sec", "env", None),
        P("sec", None, "env", None),
        P("sec", None, None, None),
        P(),
        P("sec", None),
        P("sec", "env"),
    )
    out_specs = (P("sec", "env", None), P())
    return jax.shard_map(local, mesh=mesh, in_specs=in_specs, out_specs=out_specs, check_vma=False)
```

```python
import jax
import jax.numpy as jnp
from jax import lax
from jax.experimental import pallas as pl
from jax.experimental.pallas import tpu as pltpu
from jax.sharding import PartitionSpec as P

MAXSHIFT = 2
BF = jnp.bfloat16
F32 = jnp.float32
MESH = pl.DeviceIdType.MESH
ENV = 4
LANES = 128
ZS = 8
ORDER = (1, 3, 2)


def dot(a, b):
    return jnp.dot(a, b, preferred_element_type=F32)


def make_kernel(nsec, sectors, terms, rows, cols):
    zs = ZS
    xs = nsec // (2 * zs)
    near = 2 * ENV * xs
    wide = sectors + 2 * MAXSHIFT
    half = cols // 2
    count = float(nsec * sectors * ENV * rows * cols)
    halves = (0, 1)

    def kernel(
        shifts_hbm, dims_hbm, wf_hbm, prec_hbm, left_hbm, right_hbm, out, ritz,
        shifts, dims, wf, prec, left, right,
        xs0, xs1, xd0, xd1, xq0, xq1, xt0, xt1, dall, dpad, dcols, dinv,
        live, start, va, vb, vh, vq, vc, vg, tmp, near_slots, far_slots,
        load_sem, go_sem, gi_sem, out_sem, in_sem, send_sem, d_send, d_recv,
        near_send, near_recv, far_send, far_recv, ready,
    ):
        fields = ((xs0, xs1), (xd0, xd1), (xq0, xq1))
        sec = lax.axis_index("sec")
        y = lax.axis_index("env")
        core = lax.rem(sec, 2)
        chip = sec // 2
        z = lax.rem(chip, zs)
        x = chip // zs
        has_out = jnp.logical_or(
            jnp.logical_and(core == 0, sec > 0), jnp.logical_and(core == 1, sec < nsec - 1)
        )
        outer = jnp.clip(sec + 2 * core - 1, 0, nsec - 1)
        inner = sec + 1 - 2 * core
        out_src, out_dst = 2 * core, 6 * (1 - core)
        in_src, in_dst = 2 * (1 - core), 6 * core

        def yy(k):
            return lax.rem(y + k + ENV, ENV)

        near_rank = (core * ENV + y) * xs + x

        def near_peer(k):
            m = lax.rem(near_rank + k, near)
            return (((lax.rem(m, xs) * zs + z) * 2 + m // (xs * ENV)), lax.rem(m // xs, ENV))

        def far_peer(k):
            m = lax.rem(z + k + zs, zs)
            return (((x * zs + m) * 2 + core), y)

        def x_peer(k):
            return ((lax.rem(x + k, xs) * zs + z) * 2 + core, y)

        greeted = [(sec, yy(k)) for k in range(1, ENV)] + [(inner, yy(k)) for k in range(ENV)]
        greeted += [x_peer(k) for k in range(1, xs)] + [far_peer(1), far_peer(-1)]

        loads = [
            pltpu.make_async_copy(a, b, load_sem.at[i])
            for i, (a, b) in enumerate((
                (wf_hbm, wf), (dims_hbm, dims), (prec_hbm, prec), (shifts_hbm, shifts), (left_hbm, left), (right_hbm, right),
            ))
        ]
        for load in loads:
            load.start()

        zero = jnp.zeros((MAXSHIFT, ENV, rows, half), BF)
        ones = jnp.ones((MAXSHIFT, ENV, 1, LANES), F32)

        @pl.when(sec == 0)
        def _():
            for pair in fields:
                for buf in pair:
                    buf[0:MAXSHIFT] = zero
            dall[0:MAXSHIFT] = ones

        @pl.when(sec == nsec - 1)
        def _():
            for pair in fields:
                for buf in pair:
                    buf[wide - MAXSHIFT : wide] = zero
            dall[wide - MAXSHIFT : wide] = ones

        def greet(semaphore):
            for peer in greeted:
                pl.semaphore_signal(semaphore, inc=1, device_id=peer, device_id_type=MESH)

            @pl.when(has_out)
            def _():
                pl.semaphore_signal(semaphore, inc=1, device_id=(outer, y), device_id_type=MESH)

        barrier = pltpu.get_barrier_semaphore()
        greet(barrier)
        expected = len(greeted) + jnp.where(has_out, 1, 0)

        for load in loads[:3]:
            load.wait()

        def put(pair, s, value):
            for h in halves:
                pair[h][MAXSHIFT + s, y] = value[:, h * half : (h + 1) * half].astype(BF)

        def fold(v, op=jnp.add):
            parts = [
                v[r * 8 : r * 8 + 8, c * LANES : (c + 1) * LANES]
                for r in range(rows // 8)
                for c in range(cols // LANES)
            ]
            while len(parts) > 1:
                parts = [op(a, b) for a, b in zip(parts[::2], parts[1::2], strict=True)]
            return parts[0]

        row_ids = y * rows + lax.broadcasted_iota(jnp.int32, (rows, cols), 0)
        col_ids = lax.broadcasted_iota(jnp.int32, (rows, cols), 1)
        largest = jnp.zeros((8, LANES), F32)
        for s in range(sectors):
            ok = jnp.logical_and(row_ids < dims[0, s], col_ids < dims[1, s])
            mask = jnp.where(ok, 1.0, 0.0).astype(F32)
            live[s] = mask
            st = wf[s] * mask
            start[s] = st
            put(fields[0], s, st)
            largest = jnp.maximum(largest, fold(jnp.abs(st), jnp.maximum))
            dall[MAXSHIFT + s, y, :, 0:rows] = prec[s : s + 1, :]
        dpad[...] = jnp.ones((LANES, LANES), F32)
        dpad[0:sectors, 0:rows] = prec[...]
        columns = 1.0 / jnp.transpose(dpad[...])
        for s in range(sectors):
            dinv[s] = jnp.broadcast_to(columns[0:rows, s : s + 1], (rows, LANES))
        peak = jnp.max(jnp.max(largest, axis=0, keepdims=True), axis=1, keepdims=True)
        peak = jnp.broadcast_to(jnp.where(peak > 0.0, peak, 1.0), (1, LANES))

        def across(r):
            return jnp.concatenate([r] * (cols // LANES), axis=1)

        def inverse(s):
            return jnp.concatenate([dinv[s]] * (cols // LANES), axis=1)

        pl.semaphore_wait(barrier, expected)

        def cp(src, dst, ss, rs, dev):
            return pltpu.make_async_remote_copy(
                src_ref=src, dst_ref=dst, send_sem=ss, recv_sem=rs, device_id=dev, device_id_type=MESH
            )

        def gather_outer(e, h, k):
            part = fields[e][h].at[pl.ds(MAXSHIFT + out_src, 2), y]
            return cp(part, part, send_sem.at[e, h, 0, k], go_sem.at[e, h, k], (sec, yy(k)))

        def gather_inner(e, h, k):
            part = fields[e][h].at[pl.ds(MAXSHIFT + in_src, 2), y]
            return cp(part, part, send_sem.at[e, h, 1, k], gi_sem.at[e, h, k], (sec, yy(k)))

        def relay_outer(e, h, k):
            src = fields[e][h].at[pl.ds(MAXSHIFT + out_src, 2), yy(-k)]
            dst = fields[e][h].at[pl.ds(out_dst, 2), yy(-k)]
            return cp(src, dst, send_sem.at[e, h, 2, k], out_sem.at[e, h, k], (outer, y))

        def relay_inner(e, h, k):
            src = fields[e][h].at[pl.ds(MAXSHIFT + in_src, 2), yy(-k)]
            dst = fields[e][h].at[pl.ds(in_dst, 2), yy(-k)]
            return cp(src, dst, send_sem.at[e, h, 3, k], in_sem.at[e, h, k], (inner, y))

        def begin(e, between=lambda: None):
            for h in halves:
                for k in ORDER:
                    gather_outer(e, h, k).start()
            between()

            @pl.when(has_out)
            def _():
                for h in halves:
                    relay_outer(e, h, 0).start()

            for h in halves:
                for k in ORDER:
                    gather_inner(e, h, k).start()
            for h in halves:
                relay_inner(e, h, 0).start()

        def pass_outer(e):
            for h in halves:
                for k in ORDER:
                    gather_outer(e, h, k).wait_recv()

                    @pl.when(has_out)
                    def _():
                        relay_outer(e, h, k).start()

        def pass_inner(e):
            for h in halves:
                for k in ORDER:
                    gather_inner(e, h, k).wait_recv()
                    relay_inner(e, h, k).start()

        def finish(e, h):
            @pl.when(has_out)
            def _():
                for k in (0,) + ORDER:
                    relay_outer(e, h, k).wait_recv()

            for k in (0,) + ORDER:
                relay_inner(e, h, k).wait_recv()

        def drain(e):
            for h in halves:
                for k in ORDER:
                    gather_outer(e, h, k).wait_send()
                    gather_inner(e, h, k).wait_send()
                for k in (0,) + ORDER:
                    relay_inner(e, h, k).wait_send()

                @pl.when(has_out)
                def _():
                    for k in (0,) + ORDER:
                        relay_outer(e, h, k).wait_send()

        def near_copy(r, k):
            ref = near_slots.at[r, near_rank]
            return cp(ref, ref, near_send.at[r], near_recv.at[r], near_peer(k))

        def far_copy(r, k):
            ref = far_slots.at[r, z]
            return cp(ref, ref, far_send.at[r], far_recv.at[r], far_peer(k))

        def near_all(r):
            ref = near_slots.at[r, pl.ds(0, near - 1)]
            return cp(ref, ref, near_send.at[r], near_recv.at[r], near_peer(1))

        def far_all(r):
            ref = far_slots.at[r, pl.ds(0, zs - 1)]
            return cp(ref, ref, far_send.at[r], far_recv.at[r], far_peer(1))

        lane = lax.broadcasted_iota(jnp.int32, (1, LANES), 1)
        diagonal = lax.broadcasted_iota(jnp.int32, (8, LANES), 0) == lax.broadcasted_iota(jnp.int32, (8, LANES), 1)

        def sum_begin(r, parts, last=None):
            parts = [jnp.sum(p, axis=0, keepdims=True) for p in parts]
            parts = parts + [jnp.zeros((1, LANES), F32)] * (8 - len(parts))
            each = jnp.sum(jnp.concatenate(parts, axis=0), axis=1, keepdims=True)
            packed = jnp.sum(jnp.where(diagonal, each, 0.0), axis=0, keepdims=True)
            if last is not None:
                packed = jnp.where(lane == 7, last, packed)
            near_slots[r, near_rank] = packed
            for k in range(1, near):
                near_copy(r, k).start()

        def total_of(slots, scaled):
            if not scaled:
                return jnp.sum(slots, axis=0)
            t = slots[:, 0, :]
            scale = t[:, 7:8]
            top = jnp.max(scale, axis=0, keepdims=True)
            ratio = scale / top
            t = jnp.sum(t * (ratio * ratio), axis=0, keepdims=True)
            return jnp.where(lane == 7, top, t)

        def sum_middle(r, scaled=False):
            near_all(r).wait_recv()
            far_slots[r, z] = total_of(near_slots[r], scaled)
            for k in range(1, zs):
                far_copy(r, k).start()

        def sum_end(r, scaled=False):
            far_all(r).wait_recv()
            t = total_of(far_slots[r], scaled)
            m = jnp.sum(jnp.where(diagonal, t, 0.0), axis=1, keepdims=True)
            m = jnp.broadcast_to(m, (8, LANES))
            return m * (1.0 / count), m[7:8, :]

        def sum_drain(r):
            near_all(r).wait_send()
            far_all(r).wait_send()

        def row(t, i):
            return t[i : i + 1, :]

        def h_half(pair, h, s):
            acc = jnp.zeros((rows, cols), F32)
            for w in range(terms):
                source = pair[h][s + MAXSHIFT + shifts[w]].reshape(ENV * rows, half)
                part = dot(left[s, w], source).astype(BF)
                acc = acc + dot(part, right[s, w, h * half : (h + 1) * half, :])
            return acc

        def apply_arriving(e, done):
            finish(e, 0)
            for s in range(sectors):
                tmp[s] = h_half(fields[e], 0, s)
            finish(e, 1)
            for s in range(sectors):
                done(s, (tmp[s] + h_half(fields[e], 1, s)) * live[s])

        def apply_built(dst):
            for s in range(sectors):
                dst[s] = h_half((xt0, xt1), 0, s)
            for s in range(sectors):
                dst[s] = (dst[s] + h_half((xt0, xt1), 1, s)) * live[s]

        begin(0)
        greet(ready.at[0])

        def d_copies():
            piece = dall.at[pl.ds(MAXSHIFT, sectors), y]
            res = [cp(piece, piece, d_send.at[0, k], d_recv.at[0, k], (sec, yy(k))) for k in range(1, ENV)]
            for k in range(ENV):
                src = dall.at[pl.ds(MAXSHIFT + in_src, 2), y]
                dst = dall.at[pl.ds(in_dst, 2), y]
                res.append(cp(src, dst, d_send.at[1, k], d_recv.at[1, k], (inner, yy(k))))
            return res

        def d_outer():
            res = []
            for k in range(ENV):
                src = dall.at[pl.ds(MAXSHIFT + out_src, 2), y]
                dst = dall.at[pl.ds(out_dst, 2), y]
                res.append(cp(src, dst, d_send.at[2, k], d_recv.at[2, k], (outer, yy(k))))
            return res

        for c in d_copies():
            c.start()
        pl.semaphore_wait(ready.at[0], expected)
        for k in (2, -2):
            pl.semaphore_signal(ready.at[1], inc=1, device_id=far_peer(k), device_id_type=MESH)

        @pl.when(has_out)
        def _():
            for c in d_outer():
                c.start()

        pass_outer(0)
        pass_inner(0)
        for load in loads[3:]:
            load.wait()
        inv_peak = across(1.0 / peak)
        sums = [jnp.zeros((8, LANES), F32) for _ in range(4)]

        def done0(s, a):
            di = inverse(s)
            da = a * di
            va[s] = a
            put(fields[1], s, da)
            u = start[s] * inv_peak
            ua = a * inv_peak
            for i, n in enumerate((u * u, u * ua, u * (ua * di), u * (u * di))):
                sums[i] = sums[i] + fold(n)

        apply_arriving(0, done0)

        pl.semaphore_wait(ready.at[1], 2)
        begin(1, lambda: sum_begin(1, sums, peak))
        for c in d_copies():
            c.wait_recv()

        @pl.when(has_out)
        def _():
            for c in d_outer():
                c.wait_recv()

        for s in range(wide):
            for e in range(ENV):
                dpad[s * ENV + e : s * ENV + e + 1, 0:rows] = dall[s, e, :, 0:rows]
        columns = 1.0 / jnp.transpose(dpad[...])
        for s in range(wide):
            for e in range(ENV):
                k = s * ENV + e
                dcols[s, e] = jnp.broadcast_to(columns[0:rows, k : k + 1], (rows, LANES))

        def scale_start(s, carry):
            for h in halves:
                for e in range(ENV):
                    (xt0, xt1)[h][s, e] = (fields[0][h][s, e].astype(F32) * dcols[s, e]).astype(BF)
            return carry

        lax.fori_loop(0, wide, scale_start, 0)
        apply_built(vh)
        pass_outer(1)
        sum_middle(1, True)
        pass_inner(1)

        def done1(s, b):
            vb[s] = b

        apply_arriving(1, done1)
        t, top = sum_end(1, True)
        c0 = lax.rsqrt(top * (top * row(t, 0)) + 1e-06)
        k2 = (c0 * top) * (c0 * top)
        r0, v_da0, v_dv0 = k2 * row(t, 1), k2 * row(t, 2), k2 * row(t, 3)
        along0 = v_da0 - r0 * v_dv0
        c0w, r0w, l0w = across(c0), across(r0), across(along0)
        for s in range(sectors):
            di = inverse(s)
            v, a, hd, b = start[s] * c0w, va[s] * c0w, vh[s] * c0w, vb[s] * c0w
            da = a * di
            q = b - r0w * hd - l0w * a
            corr = da - r0w * (v * di) - l0w * v
            put(fields[2], s, q * di)
            start[s], va[s], vh[s], vb[s], vq[s], vc[s] = v, a, hd, b, q, corr

        def sums_of_step():
            sums = [jnp.zeros((8, LANES), F32) for _ in range(8)]
            for s in range(sectors):
                di = inverse(s)
                v, a, q, corr = start[s], va[s], vq[s], vc[s]
                da, dq, dc = a * di, q * di, corr * di
                new = (
                    corr * corr, corr * a, v * q, corr * q,
                    v * dq + corr * da, corr * dq, v * dc, corr * dc,
                )
                sums = [c + fold(n) for c, n in zip(sums, new, strict=True)]
            sum_begin(2, sums)

        begin(2, sums_of_step)

        def build(s, carry):
            for e in range(ENV):
                di = dcols[s, e]
                for_da = c0 * di
                for_s = -for_da * (r0 * di + along0)
                for h in halves:
                    da = fields[1][h][s, e].astype(F32)
                    st = fields[0][h][s, e].astype(F32)
                    (xt0, xt1)[h][s, e] = (for_da * da + for_s * st).astype(BF)
            return carry

        lax.fori_loop(0, wide, build, 0)
        apply_built(vg)
        pass_outer(2)
        sum_middle(2)
        pass_inner(2)

        def done2(s, n):
            tmp[s] = n

        apply_arriving(2, done2)
        t, _ = sum_end(2)

        def rotation(rayleigh, upper, coupling):
            px, py = upper - rayleigh, -2.0 * coupling
            big = jnp.maximum(jnp.abs(px), jnp.abs(py))
            some = big > 0.0
            safe = jnp.where(some, big, 1.0)
            ux, uy = jnp.where(some, px / safe, 1.0), py / safe
            h = jnp.sqrt(ux * ux + uy * uy)
            large = jnp.sqrt(0.5 * (1.0 + jnp.abs(ux) / h))
            small = jnp.abs(uy) / (2.0 * h * large)
            cosine = jnp.where(ux >= 0.0, large, small)
            sine = jnp.where(ux >= 0.0, small, large)
            sine = jnp.where(uy > 0.0, sine, -sine)
            mid = 0.5 * (rayleigh - upper)
            return cosine, sine, 0.5 * (rayleigh + upper) - jnp.sqrt(mid * mid + coupling * coupling)

        alpha = lax.rsqrt(row(t, 0) + 1e-06)
        cross = row(t, 1) + row(t, 2)
        cosine, sine, value0 = rotation(r0, alpha * alpha * row(t, 3), 0.5 * alpha * cross)
        sa = sine * alpha
        r1 = cosine * cosine * r0 + cosine * sa * cross + sa * sa * row(t, 3)
        v_da = cosine * cosine * v_da0 + cosine * sa * row(t, 4) + sa * sa * row(t, 5)
        v_dv = cosine * cosine * v_dv0 + 2.0 * cosine * sa * row(t, 6) + sa * sa * row(t, 7)
        along1 = v_da - r1 * v_dv
        ritz[0:1, :] = value0
        cw, sw, r1w, l1w = across(cosine), across(sa), across(r1), across(along1)
        sums = [jnp.zeros((8, LANES), F32) for _ in range(4)]
        for s in range(sectors):
            di = inverse(s)
            v1 = cw * start[s] + sw * vc[s]
            a1 = cw * va[s] + sw * vq[s]
            c1 = (a1 - r1w * v1) * di - l1w * v1
            q1 = cw * vb[s] + sw * tmp[s] - r1w * (cw * vh[s] + sw * vg[s]) - l1w * a1
            start[s] = v1
            vc[s] = c1
            sums = [c + fold(n) for c, n in zip(sums, (c1 * c1, c1 * a1, v1 * q1, c1 * q1), strict=True)]
        sum_begin(0, sums)
        for e in range(3):
            drain(e)
        for c in d_copies():
            c.wait_send()

        @pl.when(has_out)
        def _():
            for c in d_outer():
                c.wait_send()

        sum_middle(0)
        for r in (1, 2):
            sum_drain(r)
        t, _ = sum_end(0)
        alpha = lax.rsqrt(row(t, 0) + 1e-06)
        coupling = 0.5 * alpha * (row(t, 1) + row(t, 2))
        cosine, sine, value1 = rotation(r1, alpha * alpha * row(t, 3), coupling)
        ritz[1:2, :] = value1
        cw, sw = across(cosine), across(sine * alpha)
        for s in range(sectors):
            out[s] = cw * start[s] + sw * vc[s]
        sum_drain(0)

    return kernel, near, zs, wide, half


def local(wavefunction, left_env, right_env, shifts, block_dims, precond):
    sectors, rows, cols = wavefunction.shape
    terms = left_env.shape[1]
    nsec = lax.axis_size("sec")
    kernel, near, zs, wide, half = make_kernel(nsec, sectors, terms, rows, cols)
    vmem = pl.BlockSpec(memory_space=pltpu.VMEM)
    hbm = pl.BlockSpec(memory_space=pltpu.HBM)
    held = pltpu.VMEM((wide, ENV, rows, half), BF)
    field = pltpu.VMEM((sectors, rows, cols), F32)
    dma = pltpu.SemaphoreType.DMA
    vector, ritz = pl.pallas_call(
        kernel,
        out_shape=(
            jax.ShapeDtypeStruct((sectors, rows, cols), F32),
            jax.ShapeDtypeStruct((2, LANES), F32),
        ),
        in_specs=[hbm] * 6,
        out_specs=(vmem, vmem),
        scratch_shapes=[
            pltpu.SMEM(shifts.shape, jnp.int32),
            pltpu.SMEM((2, sectors), jnp.int32),
            pltpu.VMEM(wavefunction.shape, F32),
            pltpu.VMEM(precond.shape, F32),
            pltpu.VMEM(left_env.shape, BF),
            pltpu.VMEM(right_env.shape, BF),
            held, held, held, held, held, held, held, held,
            pltpu.VMEM((wide, ENV, 1, LANES), F32),
            pltpu.VMEM((LANES, LANES), F32),
            pltpu.VMEM((wide, ENV, rows, LANES), F32),
            pltpu.VMEM((sectors, rows, LANES), F32),
            field, field, field, field, field, field, field, field, field,
            pltpu.VMEM((3, near, 1, LANES), F32),
            pltpu.VMEM((3, zs, 1, LANES), F32),
            dma((6,)),
            dma((3, 2, ENV)), dma((3, 2, ENV)), dma((3, 2, ENV)), dma((3, 2, ENV)),
            dma((3, 2, 4, ENV)),
            dma((3, ENV)), dma((3, ENV)),
            dma((3,)), dma((3,)), dma((3,)), dma((3,)),
            pltpu.SemaphoreType.REGULAR((2,)),
        ],
        compiler_params=pltpu.CompilerParams(
            collective_id=0, has_side_effects=True, vmem_limit_bytes=40 << 20
        ),
    )(*(pltpu.with_memory_space_constraint(a, pltpu.HBM) for a in (shifts, block_dims.T, wavefunction, precond, left_env, right_env)))
    return vector, ritz[:, 0]


def solution(mesh):
    in_specs = (
        P("sec", "env", None),
        P("sec", None, "env", None),
        P("sec", None, None, None),
        P(),
        P("sec", None),
        P("sec", "env"),
    )
    out_specs = (P("sec", "env", None), P())
    return jax.shard_map(local, mesh=mesh, in_specs=in_specs, out_specs=out_specs, check_vma=False)
```

```python
import jax
import jax.numpy as jnp
from jax import lax
from jax.experimental import pallas as pl
from jax.experimental.pallas import tpu as pltpu
from jax.sharding import PartitionSpec as P

MAXSHIFT = 2
BF = jnp.bfloat16
F32 = jnp.float32
MESH = pl.DeviceIdType.MESH
ENV = 4
LANES = 128
ZS = 8
ORDER = (1, 3, 2)


def dot(a, b):
    return jnp.dot(a, b, preferred_element_type=F32)


def make_kernel(nsec, sectors, terms, rows, cols):
    zs = ZS
    xs = nsec // (2 * zs)
    near = 2 * ENV * xs
    wide = sectors + 2 * MAXSHIFT
    half = cols // 2
    count = float(nsec * sectors * ENV * rows * cols)
    halves = (0, 1)

    def kernel(
        shifts_hbm, dims_hbm, wf_hbm, prec_hbm, left_hbm, right_hbm, out, ritz,
        shifts, dims, wf, prec, left, right,
        xs0, xs1, xd0, xd1, xq0, xq1, xt0, xt1, dall, dpad, dcols, dinv,
        live, start, va, vb, vh, vq, vc, vg, tmp, near_slots, far_slots,
        load_sem, go_sem, gi_sem, out_sem, in_sem, send_sem, d_send, d_recv,
        near_send, near_recv, far_send, far_recv, ready,
    ):
        fields = ((xs0, xs1), (xd0, xd1), (xq0, xq1))
        sec = lax.axis_index("sec")
        y = lax.axis_index("env")
        core = lax.rem(sec, 2)
        chip = sec // 2
        z = lax.rem(chip, zs)
        x = chip // zs
        has_out = jnp.logical_or(
            jnp.logical_and(core == 0, sec > 0), jnp.logical_and(core == 1, sec < nsec - 1)
        )
        outer = jnp.clip(sec + 2 * core - 1, 0, nsec - 1)
        inner = sec + 1 - 2 * core
        out_src, out_dst = 2 * core, 6 * (1 - core)
        in_src, in_dst = 2 * (1 - core), 6 * core

        def yy(k):
            return lax.rem(y + k + ENV, ENV)

        near_rank = (core * ENV + y) * xs + x

        def near_peer(k):
            m = lax.rem(near_rank + k, near)
            return (((lax.rem(m, xs) * zs + z) * 2 + m // (xs * ENV)), lax.rem(m // xs, ENV))

        def far_peer(k):
            m = lax.rem(z + k + zs, zs)
            return (((x * zs + m) * 2 + core), y)

        def x_peer(k):
            return ((lax.rem(x + k, xs) * zs + z) * 2 + core, y)

        greeted = [(sec, yy(k)) for k in range(1, ENV)] + [(inner, yy(k)) for k in range(ENV)]
        greeted += [x_peer(k) for k in range(1, xs)] + [far_peer(1), far_peer(-1)]

        loads = [
            pltpu.make_async_copy(a, b, load_sem.at[i])
            for i, (a, b) in enumerate((
                (wf_hbm, wf), (dims_hbm, dims), (prec_hbm, prec), (shifts_hbm, shifts), (left_hbm, left), (right_hbm, right),
            ))
        ]
        for load in loads:
            load.start()

        zero = jnp.zeros((MAXSHIFT, ENV, rows, half), BF)
        ones = jnp.ones((MAXSHIFT, ENV, 1, LANES), F32)

        @pl.when(sec == 0)
        def _():
            for pair in fields:
                for buf in pair:
                    buf[0:MAXSHIFT] = zero
            dall[0:MAXSHIFT] = ones

        @pl.when(sec == nsec - 1)
        def _():
            for pair in fields:
                for buf in pair:
                    buf[wide - MAXSHIFT : wide] = zero
            dall[wide - MAXSHIFT : wide] = ones

        def greet(semaphore):
            for peer in greeted:
                pl.semaphore_signal(semaphore, inc=1, device_id=peer, device_id_type=MESH)

            @pl.when(has_out)
            def _():
                pl.semaphore_signal(semaphore, inc=1, device_id=(outer, y), device_id_type=MESH)

        barrier = pltpu.get_barrier_semaphore()
        greet(barrier)
        expected = len(greeted) + jnp.where(has_out, 1, 0)

        for load in loads[:3]:
            load.wait()

        def put(pair, s, value):
            for h in halves:
                pair[h][MAXSHIFT + s, y] = value[:, h * half : (h + 1) * half].astype(BF)

        def fold(v, op=jnp.add):
            parts = [
                v[r * 8 : r * 8 + 8, c * LANES : (c + 1) * LANES]
                for r in range(rows // 8)
                for c in range(cols // LANES)
            ]
            while len(parts) > 1:
                parts = [op(a, b) for a, b in zip(parts[::2], parts[1::2], strict=True)]
            return parts[0]

        row_ids = y * rows + lax.broadcasted_iota(jnp.int32, (rows, cols), 0)
        col_ids = lax.broadcasted_iota(jnp.int32, (rows, cols), 1)
        largest = jnp.zeros((8, LANES), F32)
        for s in range(sectors):
            ok = jnp.logical_and(row_ids < dims[0, s], col_ids < dims[1, s])
            mask = jnp.where(ok, 1.0, 0.0).astype(F32)
            live[s] = mask
            st = wf[s] * mask
            start[s] = st
            put(fields[0], s, st)
            largest = jnp.maximum(largest, fold(jnp.abs(st), jnp.maximum))
            dall[MAXSHIFT + s, y, :, 0:rows] = prec[s : s + 1, :]
        dpad[...] = jnp.ones((LANES, LANES), F32)
        dpad[0:sectors, 0:rows] = prec[...]
        columns = 1.0 / jnp.transpose(dpad[...])
        for s in range(sectors):
            dinv[s] = jnp.broadcast_to(columns[0:rows, s : s + 1], (rows, LANES))
        peak = jnp.max(jnp.max(largest, axis=0, keepdims=True), axis=1, keepdims=True)
        peak = jnp.broadcast_to(jnp.where(peak > 0.0, peak, 1.0), (1, LANES))

        def across(r):
            return jnp.concatenate([r] * (cols // LANES), axis=1)

        def inverse(s):
            return jnp.concatenate([dinv[s]] * (cols // LANES), axis=1)

        pl.semaphore_wait(barrier, expected)

        def cp(src, dst, ss, rs, dev):
            return pltpu.make_async_remote_copy(
                src_ref=src, dst_ref=dst, send_sem=ss, recv_sem=rs, device_id=dev, device_id_type=MESH
            )

        def gather_outer(e, h, k):
            part = fields[e][h].at[pl.ds(MAXSHIFT + out_src, 2), y]
            return cp(part, part, send_sem.at[e, h, 0, k], go_sem.at[e, h, k], (sec, yy(k)))

        def gather_inner(e, h, k):
            part = fields[e][h].at[pl.ds(MAXSHIFT + in_src, 2), y]
            return cp(part, part, send_sem.at[e, h, 1, k], gi_sem.at[e, h, k], (sec, yy(k)))

        def relay_outer(e, h, k):
            src = fields[e][h].at[pl.ds(MAXSHIFT + out_src, 2), yy(-k)]
            dst = fields[e][h].at[pl.ds(out_dst, 2), yy(-k)]
            return cp(src, dst, send_sem.at[e, h, 2, k], out_sem.at[e, h, k], (outer, y))

        def relay_inner(e, h, k):
            src = fields[e][h].at[pl.ds(MAXSHIFT + in_src, 2), yy(-k)]
            dst = fields[e][h].at[pl.ds(in_dst, 2), yy(-k)]
            return cp(src, dst, send_sem.at[e, h, 3, k], in_sem.at[e, h, k], (inner, y))

        def begin_outer(e):
            for h in halves:
                for k in ORDER:
                    gather_outer(e, h, k).start()

        def begin_rest(e):
            @pl.when(has_out)
            def _():
                for h in halves:
                    relay_outer(e, h, 0).start()

            for h in halves:
                for k in ORDER:
                    gather_inner(e, h, k).start()
            for h in halves:
                relay_inner(e, h, 0).start()

        def pass_outer(e):
            for h in halves:
                for k in ORDER:
                    gather_outer(e, h, k).wait_recv()

                    @pl.when(has_out)
                    def _():
                        relay_outer(e, h, k).start()

        def pass_inner(e):
            for h in halves:
                for k in ORDER:
                    gather_inner(e, h, k).wait_recv()
                    relay_inner(e, h, k).start()

        def finish(e, h):
            @pl.when(has_out)
            def _():
                for k in (0,) + ORDER:
                    relay_outer(e, h, k).wait_recv()

            for k in (0,) + ORDER:
                relay_inner(e, h, k).wait_recv()

        def drain(e):
            for h in halves:
                for k in ORDER:
                    gather_outer(e, h, k).wait_send()
                    gather_inner(e, h, k).wait_send()
                for k in (0,) + ORDER:
                    relay_inner(e, h, k).wait_send()

                @pl.when(has_out)
                def _():
                    for k in (0,) + ORDER:
                        relay_outer(e, h, k).wait_send()

        def near_copy(r, k):
            ref = near_slots.at[r, near_rank]
            return cp(ref, ref, near_send.at[r], near_recv.at[r], near_peer(k))

        def far_copy(r, k):
            ref = far_slots.at[r, z]
            return cp(ref, ref, far_send.at[r], far_recv.at[r], far_peer(k))

        def near_all(r):
            ref = near_slots.at[r, pl.ds(0, near - 1)]
            return cp(ref, ref, near_send.at[r], near_recv.at[r], near_peer(1))

        def far_all(r):
            ref = far_slots.at[r, pl.ds(0, zs - 1)]
            return cp(ref, ref, far_send.at[r], far_recv.at[r], far_peer(1))

        lane = lax.broadcasted_iota(jnp.int32, (1, LANES), 1)
        diagonal = lax.broadcasted_iota(jnp.int32, (8, LANES), 0) == lax.broadcasted_iota(jnp.int32, (8, LANES), 1)

        def sum_begin(r, parts, last=None):
            parts = [jnp.sum(p, axis=0, keepdims=True) for p in parts]
            parts = parts + [jnp.zeros((1, LANES), F32)] * (8 - len(parts))
            each = jnp.sum(jnp.concatenate(parts, axis=0), axis=1, keepdims=True)
            packed = jnp.sum(jnp.where(diagonal, each, 0.0), axis=0, keepdims=True)
            if last is not None:
                packed = jnp.where(lane == 7, last, packed)
            near_slots[r, near_rank] = packed
            for k in range(1, near):
                near_copy(r, k).start()

        def total_of(slots, scaled):
            if not scaled:
                return jnp.sum(slots, axis=0)
            t = slots[:, 0, :]
            scale = t[:, 7:8]
            top = jnp.max(scale, axis=0, keepdims=True)
            ratio = scale / top
            t = jnp.sum(t * (ratio * ratio), axis=0, keepdims=True)
            return jnp.where(lane == 7, top, t)

        def sum_middle(r, scaled=False):
            near_all(r).wait_recv()
            far_slots[r, z] = total_of(near_slots[r], scaled)
            for k in range(1, zs):
                far_copy(r, k).start()

        def sum_end(r, scaled=False):
            far_all(r).wait_recv()
            t = total_of(far_slots[r], scaled)
            m = jnp.sum(jnp.where(diagonal, t, 0.0), axis=1, keepdims=True)
            m = jnp.broadcast_to(m, (8, LANES))
            return m * (1.0 / count), m[7:8, :]

        def sum_drain(r):
            near_all(r).wait_send()
            far_all(r).wait_send()

        def row(t, i):
            return t[i : i + 1, :]

        def h_half(pair, h, s):
            acc = jnp.zeros((rows, cols), F32)
            for w in range(terms):
                source = pair[h][s + MAXSHIFT + shifts[w]].reshape(ENV * rows, half)
                part = dot(left[s, w], source).astype(BF)
                acc = acc + dot(part, right[s, w, h * half : (h + 1) * half, :])
            return acc

        def apply_arriving(e, prepare, settle):
            finish(e, 0)
            for s in range(sectors):
                tmp[s] = h_half(fields[e], 0, s)
            finish(e, 1)
            for first in (out_src, in_src):
                for j in range(2):
                    s = first + j
                    tmp[s] = (tmp[s] + h_half(fields[e], 1, s)) * live[s]
                if first is out_src:
                    prepare()
                for j in range(2):
                    settle(first + j, tmp[first + j])
                if first is out_src:
                    begin_outer(e + 1)

        def apply_built(dst):
            for s in range(sectors):
                dst[s] = h_half((xt0, xt1), 0, s)
            for s in range(sectors):
                dst[s] = (dst[s] + h_half((xt0, xt1), 1, s)) * live[s]

        begin_outer(0)
        begin_rest(0)
        greet(ready.at[0])

        def d_copies():
            piece = dall.at[pl.ds(MAXSHIFT, sectors), y]
            res = [cp(piece, piece, d_send.at[0, k], d_recv.at[0, k], (sec, yy(k))) for k in range(1, ENV)]
            for k in range(ENV):
                src = dall.at[pl.ds(MAXSHIFT + in_src, 2), y]
                dst = dall.at[pl.ds(in_dst, 2), y]
                res.append(cp(src, dst, d_send.at[1, k], d_recv.at[1, k], (inner, yy(k))))
            return res

        def d_outer():
            res = []
            for k in range(ENV):
                src = dall.at[pl.ds(MAXSHIFT + out_src, 2), y]
                dst = dall.at[pl.ds(out_dst, 2), y]
                res.append(cp(src, dst, d_send.at[2, k], d_recv.at[2, k], (outer, yy(k))))
            return res

        for c in d_copies():
            c.start()
        pl.semaphore_wait(ready.at[0], expected)
        for k in (2, -2):
            pl.semaphore_signal(ready.at[1], inc=1, device_id=far_peer(k), device_id_type=MESH)

        @pl.when(has_out)
        def _():
            for c in d_outer():
                c.start()

        pass_outer(0)
        pass_inner(0)
        for load in loads[3:]:
            load.wait()
        inv_peak = across(1.0 / peak)
        sums = [jnp.zeros((8, LANES), F32) for _ in range(4)]

        def done0(s, a):
            di = inverse(s)
            da = a * di
            va[s] = a
            put(fields[1], s, da)
            u = start[s] * inv_peak
            ua = a * inv_peak
            for i, n in enumerate((u * u, u * ua, u * (ua * di), u * (u * di))):
                sums[i] = sums[i] + fold(n)

        apply_arriving(0, lambda: None, done0)

        pl.semaphore_wait(ready.at[1], 2)
        sum_begin(1, sums, peak)
        begin_rest(1)
        for c in d_copies():
            c.wait_recv()

        @pl.when(has_out)
        def _():
            for c in d_outer():
                c.wait_recv()

        for s in range(wide):
            for e in range(ENV):
                dpad[s * ENV + e : s * ENV + e + 1, 0:rows] = dall[s, e, :, 0:rows]
        columns = 1.0 / jnp.transpose(dpad[...])
        for s in range(wide):
            for e in range(ENV):
                k = s * ENV + e
                dcols[s, e] = jnp.broadcast_to(columns[0:rows, k : k + 1], (rows, LANES))

        def scale_start(s, carry):
            for h in halves:
                for e in range(ENV):
                    (xt0, xt1)[h][s, e] = (fields[0][h][s, e].astype(F32) * dcols[s, e]).astype(BF)
            return carry

        lax.fori_loop(0, wide, scale_start, 0)
        apply_built(vh)
        pass_outer(1)
        sum_middle(1, True)
        pass_inner(1)

        first_step = {}

        def scalars_of_start():
            t, top = sum_end(1, True)
            c0 = lax.rsqrt(top * (top * row(t, 0)) + 1e-06)
            k2 = (c0 * top) * (c0 * top)
            r0, v_da0, v_dv0 = k2 * row(t, 1), k2 * row(t, 2), k2 * row(t, 3)
            first_step["scalars"] = c0, r0, v_da0 - r0 * v_dv0, v_da0, v_dv0

        def done1(s, b):
            c0w, r0w, l0w = (across(c) for c in first_step["scalars"][:3])
            di = inverse(s)
            v, a, hd, b = start[s] * c0w, va[s] * c0w, vh[s] * c0w, b * c0w
            q = b - r0w * hd - l0w * a
            put(fields[2], s, q * di)
            corr = a * di - r0w * (v * di) - l0w * v
            start[s], va[s], vh[s], vb[s], vq[s], vc[s] = v, a, hd, b, q, corr

        apply_arriving(1, scalars_of_start, done1)
        c0, r0, along0, v_da0, v_dv0 = first_step["scalars"]

        sums = [jnp.zeros((8, LANES), F32) for _ in range(8)]
        for s in range(sectors):
            di = inverse(s)
            v, a, q, corr = start[s], va[s], vq[s], vc[s]
            da, dq, dc = a * di, q * di, corr * di
            new = (
                corr * corr, corr * a, v * q, corr * q,
                v * dq + corr * da, corr * dq, v * dc, corr * dc,
            )
            sums = [c + fold(n) for c, n in zip(sums, new, strict=True)]
        sum_begin(2, sums)
        begin_rest(2)

        def build(s, carry):
            for e in range(ENV):
                di = dcols[s, e]
                for_da = c0 * di
                for_s = -for_da * (r0 * di + along0)
                for h in halves:
                    da = fields[1][h][s, e].astype(F32)
                    st = fields[0][h][s, e].astype(F32)
                    (xt0, xt1)[h][s, e] = (for_da * da + for_s * st).astype(BF)
            return carry

        lax.fori_loop(0, wide, build, 0)
        apply_built(vg)
        pass_outer(2)
        sum_middle(2)
        pass_inner(2)

        for h in halves:
            finish(2, h)
            for s in range(sectors):
                n = h_half(fields[2], h, s)
                tmp[s] = n if h == 0 else (tmp[s] + n) * live[s]
        t, _ = sum_end(2)

        def rotation(rayleigh, upper, coupling):
            px, py = upper - rayleigh, -2.0 * coupling
            big = jnp.maximum(jnp.abs(px), jnp.abs(py))
            some = big > 0.0
            safe = jnp.where(some, big, 1.0)
            ux, uy = jnp.where(some, px / safe, 1.0), py / safe
            h = jnp.sqrt(ux * ux + uy * uy)
            large = jnp.sqrt(0.5 * (1.0 + jnp.abs(ux) / h))
            small = jnp.abs(uy) / (2.0 * h * large)
            cosine = jnp.where(ux >= 0.0, large, small)
            sine = jnp.where(ux >= 0.0, small, large)
            sine = jnp.where(uy > 0.0, sine, -sine)
            mid = 0.5 * (rayleigh - upper)
            return cosine, sine, 0.5 * (rayleigh + upper) - jnp.sqrt(mid * mid + coupling * coupling)

        alpha = lax.rsqrt(row(t, 0) + 1e-06)
        cross = row(t, 1) + row(t, 2)
        cosine, sine, value0 = rotation(r0, alpha * alpha * row(t, 3), 0.5 * alpha * cross)
        sa = sine * alpha
        r1 = cosine * cosine * r0 + cosine * sa * cross + sa * sa * row(t, 3)
        v_da = cosine * cosine * v_da0 + cosine * sa * row(t, 4) + sa * sa * row(t, 5)
        v_dv = cosine * cosine * v_dv0 + 2.0 * cosine * sa * row(t, 6) + sa * sa * row(t, 7)
        along1 = v_da - r1 * v_dv
        ritz[0:1, :] = value0
        cw, sw, r1w, l1w = across(cosine), across(sa), across(r1), across(along1)
        sums = [jnp.zeros((8, LANES), F32) for _ in range(4)]
        for s in range(sectors):
            di = inverse(s)
            v1 = cw * start[s] + sw * vc[s]
            a1 = cw * va[s] + sw * vq[s]
            c1 = (a1 - r1w * v1) * di - l1w * v1
            q1 = cw * vb[s] + sw * tmp[s] - r1w * (cw * vh[s] + sw * vg[s]) - l1w * a1
            start[s] = v1
            vc[s] = c1
            sums = [c + fold(n) for c, n in zip(sums, (c1 * c1, c1 * a1, v1 * q1, c1 * q1), strict=True)]
        sum_begin(0, sums)
        for e in range(3):
            drain(e)
        for c in d_copies():
            c.wait_send()

        @pl.when(has_out)
        def _():
            for c in d_outer():
                c.wait_send()

        sum_middle(0)
        for r in (1, 2):
            sum_drain(r)
        t, _ = sum_end(0)
        alpha = lax.rsqrt(row(t, 0) + 1e-06)
        coupling = 0.5 * alpha * (row(t, 1) + row(t, 2))
        cosine, sine, value1 = rotation(r1, alpha * alpha * row(t, 3), coupling)
        ritz[1:2, :] = value1
        cw, sw = across(cosine), across(sine * alpha)
        for s in range(sectors):
            out[s] = cw * start[s] + sw * vc[s]
        sum_drain(0)

    return kernel, near, zs, wide, half


def local(wavefunction, left_env, right_env, shifts, block_dims, precond):
    sectors, rows, cols = wavefunction.shape
    terms = left_env.shape[1]
    nsec = lax.axis_size("sec")
    kernel, near, zs, wide, half = make_kernel(nsec, sectors, terms, rows, cols)
    vmem = pl.BlockSpec(memory_space=pltpu.VMEM)
    hbm = pl.BlockSpec(memory_space=pltpu.HBM)
    held = pltpu.VMEM((wide, ENV, rows, half), BF)
    field = pltpu.VMEM((sectors, rows, cols), F32)
    dma = pltpu.SemaphoreType.DMA
    vector, ritz = pl.pallas_call(
        kernel,
        out_shape=(
            jax.ShapeDtypeStruct((sectors, rows, cols), F32),
            jax.ShapeDtypeStruct((2, LANES), F32),
        ),
        in_specs=[hbm] * 6,
        out_specs=(vmem, vmem),
        scratch_shapes=[
            pltpu.SMEM(shifts.shape, jnp.int32),
            pltpu.SMEM((2, sectors), jnp.int32),
            pltpu.VMEM(wavefunction.shape, F32),
            pltpu.VMEM(precond.shape, F32),
            pltpu.VMEM(left_env.shape, BF),
            pltpu.VMEM(right_env.shape, BF),
            held, held, held, held, held, held, held, held,
            pltpu.VMEM((wide, ENV, 1, LANES), F32),
            pltpu.VMEM((LANES, LANES), F32),
            pltpu.VMEM((wide, ENV, rows, LANES), F32),
            pltpu.VMEM((sectors, rows, LANES), F32),
            field, field, field, field, field, field, field, field, field,
            pltpu.VMEM((3, near, 1, LANES), F32),
            pltpu.VMEM((3, zs, 1, LANES), F32),
            dma((6,)),
            dma((3, 2, ENV)), dma((3, 2, ENV)), dma((3, 2, ENV)), dma((3, 2, ENV)),
            dma((3, 2, 4, ENV)),
            dma((3, ENV)), dma((3, ENV)),
            dma((3,)), dma((3,)), dma((3,)), dma((3,)),
            pltpu.SemaphoreType.REGULAR((2,)),
        ],
        compiler_params=pltpu.CompilerParams(
            collective_id=0, has_side_effects=True, vmem_limit_bytes=40 << 20
        ),
    )(*(pltpu.with_memory_space_constraint(a, pltpu.HBM) for a in (shifts, block_dims.T, wavefunction, precond, left_env, right_env)))
    return vector, ritz[:, 0]


def solution(mesh):
    in_specs = (
        P("sec", "env", None),
        P("sec", None, "env", None),
        P("sec", None, None, None),
        P(),
        P("sec", None),
        P("sec", "env"),
    )
    out_specs = (P("sec", "env", None), P())
    return jax.shard_map(local, mesh=mesh, in_specs=in_specs, out_specs=out_specs, check_vma=False)
```

```python
import jax
import jax.numpy as jnp
from jax import lax
from jax.experimental import pallas as pl
from jax.experimental.pallas import tpu as pltpu
from jax.sharding import PartitionSpec as P

MAXSHIFT = 2
BF = jnp.bfloat16
F32 = jnp.float32
MESH = pl.DeviceIdType.MESH
ENV = 4
LANES = 128
ZS = 8
ORDER = (1, 3, 2)


def dot(a, b):
    return jnp.dot(a, b, preferred_element_type=F32)


def make_kernel(nsec, sectors, terms, rows, cols):
    zs = ZS
    xs = nsec // (2 * zs)
    near = 2 * ENV * xs
    wide = sectors + 2 * MAXSHIFT
    half = cols // 2
    count = float(nsec * sectors * ENV * rows * cols)
    halves = (0, 1)

    def kernel(
        shifts_hbm, dims_hbm, wf_hbm, prec_hbm, left_hbm, right_hbm, out, ritz,
        shifts, dims, wf, prec, left, right,
        xs0, xs1, xd0, xd1, xq0, xq1, xt0, xt1, dall, dpad, dcols, dinv,
        live, start, va, vb, vh, vq, vc, vg, tmp, near_slots, far_slots,
        load_sem, go_sem, gi_sem, out_sem, in_sem, send_sem, d_send, d_recv,
        near_send, near_recv, far_send, far_recv, ready,
    ):
        fields = ((xs0, xs1), (xd0, xd1), (xq0, xq1))
        sec = lax.axis_index("sec")
        y = lax.axis_index("env")
        core = lax.rem(sec, 2)
        chip = sec // 2
        z = lax.rem(chip, zs)
        x = chip // zs
        has_out = jnp.logical_or(
            jnp.logical_and(core == 0, sec > 0), jnp.logical_and(core == 1, sec < nsec - 1)
        )
        outer = jnp.clip(sec + 2 * core - 1, 0, nsec - 1)
        inner = sec + 1 - 2 * core
        out_src, out_dst = 2 * core, 6 * (1 - core)
        in_src, in_dst = 2 * (1 - core), 6 * core

        def yy(k):
            return lax.rem(y + k + ENV, ENV)

        near_rank = (core * ENV + y) * xs + x

        shifted_x = [lax.rem(x + d, xs) for d in range(xs)]
        shifted_y = [lax.rem(y + d, ENV) for d in range(ENV)]
        offsets = [(c, dy, dx) for dx in range(xs) for dy in range(ENV) for c in (0, 1)][1:]
        offsets.sort(key=lambda o: -(min(o[1], ENV - o[1]) + min(o[2], xs - o[2])))

        def near_peer(k):
            c, dy, dx = offsets[k - 1]
            other = core if c == 0 else 1 - core
            return ((shifted_x[dx] * zs + z) * 2 + other, shifted_y[dy])

        def far_peer(k):
            m = lax.rem(z + k + zs, zs)
            return (((x * zs + m) * 2 + core), y)

        def x_peer(k):
            return ((lax.rem(x + k, xs) * zs + z) * 2 + core, y)

        greeted = [(sec, yy(k)) for k in range(1, ENV)] + [(inner, yy(k)) for k in range(ENV)]
        greeted += [x_peer(k) for k in range(1, xs)] + [far_peer(1), far_peer(-1)]

        zero = jnp.zeros((MAXSHIFT, ENV, rows, half), BF)
        ones = jnp.ones((MAXSHIFT, ENV, 1, LANES), F32)

        @pl.when(sec == 0)
        def _():
            for pair in fields:
                for buf in pair:
                    buf[0:MAXSHIFT] = zero
            dall[0:MAXSHIFT] = ones

        @pl.when(sec == nsec - 1)
        def _():
            for pair in fields:
                for buf in pair:
                    buf[wide - MAXSHIFT : wide] = zero
            dall[wide - MAXSHIFT : wide] = ones

        def greet(semaphore):
            for peer in greeted:
                pl.semaphore_signal(semaphore, inc=1, device_id=peer, device_id_type=MESH)

            @pl.when(has_out)
            def _():
                pl.semaphore_signal(semaphore, inc=1, device_id=(outer, y), device_id_type=MESH)

        barrier = pltpu.get_barrier_semaphore()
        greet(barrier)
        expected = len(greeted) + jnp.where(has_out, 1, 0)

        loads = [
            pltpu.make_async_copy(a, b, load_sem.at[i])
            for i, (a, b) in enumerate((
                (wf_hbm, wf), (dims_hbm, dims), (prec_hbm, prec), (shifts_hbm, shifts), (left_hbm, left), (right_hbm, right),
            ))
        ]
        for load in loads:
            load.start()

        for load in loads[:3]:
            load.wait()

        def put(pair, s, value):
            for h in halves:
                pair[h][MAXSHIFT + s, y] = value[:, h * half : (h + 1) * half].astype(BF)

        def fold(v, op=jnp.add):
            parts = [
                v[r * 8 : r * 8 + 8, c * LANES : (c + 1) * LANES]
                for r in range(rows // 8)
                for c in range(cols // LANES)
            ]
            while len(parts) > 1:
                parts = [op(a, b) for a, b in zip(parts[::2], parts[1::2], strict=True)]
            return parts[0]

        row_ids = y * rows + lax.broadcasted_iota(jnp.int32, (rows, cols), 0)
        col_ids = lax.broadcasted_iota(jnp.int32, (rows, cols), 1)
        largest = jnp.zeros((8, LANES), F32)
        for s in range(sectors):
            ok = jnp.logical_and(row_ids < dims[0, s], col_ids < dims[1, s])
            mask = jnp.where(ok, 1.0, 0.0).astype(F32)
            live[s] = mask
            st = wf[s] * mask
            start[s] = st
            put(fields[0], s, st)
            largest = jnp.maximum(largest, fold(jnp.abs(st), jnp.maximum))
            dall[MAXSHIFT + s, y, :, 0:rows] = prec[s : s + 1, :]
        dpad[...] = jnp.ones((LANES, LANES), F32)
        dpad[0:sectors, 0:rows] = prec[...]
        columns = 1.0 / jnp.transpose(dpad[...])
        for s in range(sectors):
            dinv[s] = jnp.broadcast_to(columns[0:rows, s : s + 1], (rows, LANES))
        peak = jnp.max(jnp.max(largest, axis=0, keepdims=True), axis=1, keepdims=True)
        peak = jnp.broadcast_to(jnp.where(peak > 0.0, peak, 1.0), (1, LANES))

        def across(r):
            return jnp.concatenate([r] * (cols // LANES), axis=1)

        def inverse(s):
            return jnp.concatenate([dinv[s]] * (cols // LANES), axis=1)

        pl.semaphore_wait(barrier, expected)

        def cp(src, dst, ss, rs, dev):
            return pltpu.make_async_remote_copy(
                src_ref=src, dst_ref=dst, send_sem=ss, recv_sem=rs, device_id=dev, device_id_type=MESH
            )

        def gather_outer(e, h, k):
            part = fields[e][h].at[pl.ds(MAXSHIFT + out_src, 2), y]
            return cp(part, part, send_sem.at[e, h, 0, k], go_sem.at[e, h, k], (sec, yy(k)))

        def gather_inner(e, h, k):
            part = fields[e][h].at[pl.ds(MAXSHIFT + in_src, 2), y]
            return cp(part, part, send_sem.at[e, h, 1, k], gi_sem.at[e, h, k], (sec, yy(k)))

        def relay_outer(e, h, k):
            src = fields[e][h].at[pl.ds(MAXSHIFT + out_src, 2), yy(-k)]
            dst = fields[e][h].at[pl.ds(out_dst, 2), yy(-k)]
            return cp(src, dst, send_sem.at[e, h, 2, k], out_sem.at[e, h, k], (outer, y))

        def relay_inner(e, h, k):
            src = fields[e][h].at[pl.ds(MAXSHIFT + in_src, 2), yy(-k)]
            dst = fields[e][h].at[pl.ds(in_dst, 2), yy(-k)]
            return cp(src, dst, send_sem.at[e, h, 3, k], in_sem.at[e, h, k], (inner, y))

        def begin_outer(e):
            for h in halves:
                for k in ORDER:
                    gather_outer(e, h, k).start()

        def begin_rest(e):
            @pl.when(has_out)
            def _():
                for h in halves:
                    relay_outer(e, h, 0).start()

            for h in halves:
                for k in ORDER:
                    gather_inner(e, h, k).start()
            for h in halves:
                relay_inner(e, h, 0).start()

        def pass_outer(e):
            for h in halves:
                for k in ORDER:
                    gather_outer(e, h, k).wait_recv()

                    @pl.when(has_out)
                    def _():
                        relay_outer(e, h, k).start()

        def pass_inner(e):
            for h in halves:
                for k in ORDER:
                    gather_inner(e, h, k).wait_recv()
                    relay_inner(e, h, k).start()

        def finish(e, h):
            @pl.when(has_out)
            def _():
                for k in (0,) + ORDER:
                    relay_outer(e, h, k).wait_recv()

            for k in (0,) + ORDER:
                relay_inner(e, h, k).wait_recv()

        def drain(e):
            for h in halves:
                for k in ORDER:
                    gather_outer(e, h, k).wait_send()
                    gather_inner(e, h, k).wait_send()
                for k in (0,) + ORDER:
                    relay_inner(e, h, k).wait_send()

                @pl.when(has_out)
                def _():
                    for k in (0,) + ORDER:
                        relay_outer(e, h, k).wait_send()

        def near_copy(r, k):
            ref = near_slots.at[r, near_rank]
            return cp(ref, ref, near_send.at[r], near_recv.at[r], near_peer(k))

        def far_copy(r, k):
            ref = far_slots.at[r, z]
            return cp(ref, ref, far_send.at[r], far_recv.at[r], far_peer(k))

        def near_all(r):
            ref = near_slots.at[r, pl.ds(0, near - 1)]
            return cp(ref, ref, near_send.at[r], near_recv.at[r], near_peer(1))

        def far_all(r):
            ref = far_slots.at[r, pl.ds(0, zs - 1)]
            return cp(ref, ref, far_send.at[r], far_recv.at[r], far_peer(1))

        lane = lax.broadcasted_iota(jnp.int32, (1, LANES), 1)
        diagonal = lax.broadcasted_iota(jnp.int32, (8, LANES), 0) == lax.broadcasted_iota(jnp.int32, (8, LANES), 1)

        def sum_begin(r, parts, last=None):
            parts = [jnp.sum(p, axis=0, keepdims=True) for p in parts]
            parts = parts + [jnp.zeros((1, LANES), F32)] * (8 - len(parts))
            each = jnp.sum(jnp.concatenate(parts, axis=0), axis=1, keepdims=True)
            packed = jnp.sum(jnp.where(diagonal, each, 0.0), axis=0, keepdims=True)
            if last is not None:
                packed = jnp.where(lane == 7, last, packed)
            near_slots[r, near_rank] = packed
            for k in range(1, near):
                near_copy(r, k).start()

        def total_of(slots, scaled):
            if not scaled:
                return jnp.sum(slots, axis=0)
            t = slots[:, 0, :]
            scale = t[:, 7:8]
            top = jnp.max(scale, axis=0, keepdims=True)
            ratio = scale / top
            t = jnp.sum(t * (ratio * ratio), axis=0, keepdims=True)
            return jnp.where(lane == 7, top, t)

        def sum_middle(r, scaled=False):
            near_all(r).wait_recv()
            far_slots[r, z] = total_of(near_slots[r], scaled)
            for k in range(1, zs):
                far_copy(r, k).start()

        def sum_end(r, scaled=False):
            far_all(r).wait_recv()
            t = total_of(far_slots[r], scaled)
            m = jnp.sum(jnp.where(diagonal, t, 0.0), axis=1, keepdims=True)
            m = jnp.broadcast_to(m, (8, LANES))
            return m * (1.0 / count), m[7:8, :]

        def sum_drain(r):
            near_all(r).wait_send()
            far_all(r).wait_send()

        def row(t, i):
            return t[i : i + 1, :]

        def h_half(pair, h, s):
            acc = jnp.zeros((rows, cols), F32)
            for w in range(terms):
                source = pair[h][s + MAXSHIFT + shifts[w]].reshape(ENV * rows, half)
                part = dot(left[s, w], source).astype(BF)
                acc = acc + dot(part, right[s, w, h * half : (h + 1) * half, :])
            return acc

        def apply_arriving(e, prepare, settle):
            finish(e, 0)
            for s in range(sectors):
                tmp[s] = h_half(fields[e], 0, s)
            finish(e, 1)
            for first in (out_src, in_src):
                for j in range(2):
                    s = first + j
                    tmp[s] = (tmp[s] + h_half(fields[e], 1, s)) * live[s]
                if first is out_src:
                    prepare()
                for j in range(2):
                    settle(first + j, tmp[first + j])
                if first is out_src:
                    begin_outer(e + 1)

        def apply_built(dst):
            for s in range(sectors):
                dst[s] = h_half((xt0, xt1), 0, s)
            for s in range(sectors):
                dst[s] = (dst[s] + h_half((xt0, xt1), 1, s)) * live[s]

        begin_outer(0)
        begin_rest(0)
        greet(ready.at[0])

        def d_copies():
            piece = dall.at[pl.ds(MAXSHIFT, sectors), y]
            res = [cp(piece, piece, d_send.at[0, k], d_recv.at[0, k], (sec, yy(k))) for k in range(1, ENV)]
            for k in range(ENV):
                src = dall.at[pl.ds(MAXSHIFT + in_src, 2), y]
                dst = dall.at[pl.ds(in_dst, 2), y]
                res.append(cp(src, dst, d_send.at[1, k], d_recv.at[1, k], (inner, yy(k))))
            return res

        def d_outer():
            res = []
            for k in range(ENV):
                src = dall.at[pl.ds(MAXSHIFT + out_src, 2), y]
                dst = dall.at[pl.ds(out_dst, 2), y]
                res.append(cp(src, dst, d_send.at[2, k], d_recv.at[2, k], (outer, yy(k))))
            return res

        for c in d_copies():
            c.start()
        pl.semaphore_wait(ready.at[0], expected)
        for k in (2, -2):
            pl.semaphore_signal(ready.at[1], inc=1, device_id=far_peer(k), device_id_type=MESH)

        @pl.when(has_out)
        def _():
            for c in d_outer():
                c.start()

        pass_outer(0)
        pass_inner(0)
        for load in loads[3:]:
            load.wait()
        inv_peak = across(1.0 / peak)
        sums = [jnp.zeros((8, LANES), F32) for _ in range(4)]

        def done0(s, a):
            di = inverse(s)
            da = a * di
            va[s] = a
            put(fields[1], s, da)
            u = start[s] * inv_peak
            ua = a * inv_peak
            for i, n in enumerate((u * u, u * ua, u * (ua * di), u * (u * di))):
                sums[i] = sums[i] + fold(n)

        apply_arriving(0, lambda: None, done0)

        pl.semaphore_wait(ready.at[1], 2)
        sum_begin(1, sums, peak)
        begin_rest(1)
        for c in d_copies():
            c.wait_recv()

        @pl.when(has_out)
        def _():
            for c in d_outer():
                c.wait_recv()

        for s in range(wide):
            for e in range(ENV):
                dpad[s * ENV + e : s * ENV + e + 1, 0:rows] = dall[s, e, :, 0:rows]
        columns = 1.0 / jnp.transpose(dpad[...])
        for s in range(wide):
            for e in range(ENV):
                k = s * ENV + e
                dcols[s, e] = jnp.broadcast_to(columns[0:rows, k : k + 1], (rows, LANES))

        def scale_start(s, carry):
            for h in halves:
                for e in range(ENV):
                    (xt0, xt1)[h][s, e] = (fields[0][h][s, e].astype(F32) * dcols[s, e]).astype(BF)
            return carry

        lax.fori_loop(0, wide, scale_start, 0)
        apply_built(vh)
        pass_outer(1)
        sum_middle(1, True)
        pass_inner(1)

        first_step = {}

        def scalars_of_start():
            t, top = sum_end(1, True)
            c0 = lax.rsqrt(top * (top * row(t, 0)) + 1e-06)
            k2 = (c0 * top) * (c0 * top)
            r0, v_da0, v_dv0 = k2 * row(t, 1), k2 * row(t, 2), k2 * row(t, 3)
            first_step["scalars"] = c0, r0, v_da0 - r0 * v_dv0, v_da0, v_dv0

        def done1(s, b):
            c0w, r0w, l0w = (across(c) for c in first_step["scalars"][:3])
            di = inverse(s)
            v, a, hd, b = start[s] * c0w, va[s] * c0w, vh[s] * c0w, b * c0w
            q = b - r0w * hd - l0w * a
            put(fields[2], s, q * di)
            corr = a * di - r0w * (v * di) - l0w * v
            start[s], va[s], vh[s], vb[s], vq[s], vc[s] = v, a, hd, b, q, corr

        apply_arriving(1, scalars_of_start, done1)
        c0, r0, along0, v_da0, v_dv0 = first_step["scalars"]

        sums = [jnp.zeros((8, LANES), F32) for _ in range(8)]
        for s in range(sectors):
            di = inverse(s)
            v, a, q, corr = start[s], va[s], vq[s], vc[s]
            da, dq, dc = a * di, q * di, corr * di
            new = (
                corr * corr, corr * a, v * q, corr * q,
                v * dq + corr * da, corr * dq, v * dc, corr * dc,
            )
            sums = [c + fold(n) for c, n in zip(sums, new, strict=True)]
        sum_begin(2, sums)
        begin_rest(2)

        def build(s, carry):
            for e in range(ENV):
                di = dcols[s, e]
                for_da = c0 * di
                for_s = -for_da * (r0 * di + along0)
                for h in halves:
                    da = fields[1][h][s, e].astype(F32)
                    st = fields[0][h][s, e].astype(F32)
                    (xt0, xt1)[h][s, e] = (for_da * da + for_s * st).astype(BF)
            return carry

        lax.fori_loop(0, wide, build, 0)
        apply_built(vg)
        pass_outer(2)
        sum_middle(2)
        pass_inner(2)

        for h in halves:
            finish(2, h)
            for s in range(sectors):
                n = h_half(fields[2], h, s)
                tmp[s] = n if h == 0 else (tmp[s] + n) * live[s]
        t, _ = sum_end(2)

        def rotation(rayleigh, upper, coupling):
            px, py = upper - rayleigh, -2.0 * coupling
            big = jnp.maximum(jnp.abs(px), jnp.abs(py))
            some = big > 0.0
            safe = jnp.where(some, big, 1.0)
            ux, uy = jnp.where(some, px / safe, 1.0), py / safe
            h = jnp.sqrt(ux * ux + uy * uy)
            large = jnp.sqrt(0.5 * (1.0 + jnp.abs(ux) / h))
            small = jnp.abs(uy) / (2.0 * h * large)
            cosine = jnp.where(ux >= 0.0, large, small)
            sine = jnp.where(ux >= 0.0, small, large)
            sine = jnp.where(uy > 0.0, sine, -sine)
            mid = 0.5 * (rayleigh - upper)
            return cosine, sine, 0.5 * (rayleigh + upper) - jnp.sqrt(mid * mid + coupling * coupling)

        alpha = lax.rsqrt(row(t, 0) + 1e-06)
        cross = row(t, 1) + row(t, 2)
        cosine, sine, value0 = rotation(r0, alpha * alpha * row(t, 3), 0.5 * alpha * cross)
        sa = sine * alpha
        r1 = cosine * cosine * r0 + cosine * sa * cross + sa * sa * row(t, 3)
        v_da = cosine * cosine * v_da0 + cosine * sa * row(t, 4) + sa * sa * row(t, 5)
        v_dv = cosine * cosine * v_dv0 + 2.0 * cosine * sa * row(t, 6) + sa * sa * row(t, 7)
        along1 = v_da - r1 * v_dv
        ritz[0:1, :] = value0
        cw, sw, r1w, l1w = across(cosine), across(sa), across(r1), across(along1)
        sums = [jnp.zeros((8, LANES), F32) for _ in range(4)]
        for s in range(sectors):
            di = inverse(s)
            v1 = cw * start[s] + sw * vc[s]
            a1 = cw * va[s] + sw * vq[s]
            c1 = (a1 - r1w * v1) * di - l1w * v1
            q1 = cw * vb[s] + sw * tmp[s] - r1w * (cw * vh[s] + sw * vg[s]) - l1w * a1
            start[s] = v1
            vc[s] = c1
            sums = [c + fold(n) for c, n in zip(sums, (c1 * c1, c1 * a1, v1 * q1, c1 * q1), strict=True)]
        sum_begin(0, sums)
        for e in range(3):
            drain(e)
        for c in d_copies():
            c.wait_send()

        @pl.when(has_out)
        def _():
            for c in d_outer():
                c.wait_send()

        sum_middle(0)
        for r in (1, 2):
            sum_drain(r)
        t, _ = sum_end(0)
        alpha = lax.rsqrt(row(t, 0) + 1e-06)
        coupling = 0.5 * alpha * (row(t, 1) + row(t, 2))
        cosine, sine, value1 = rotation(r1, alpha * alpha * row(t, 3), coupling)
        ritz[1:2, :] = value1
        cw, sw = across(cosine), across(sine * alpha)
        for s in range(sectors):
            out[s] = cw * start[s] + sw * vc[s]
        sum_drain(0)

    return kernel, near, zs, wide, half


def local(wavefunction, left_env, right_env, shifts, block_dims, precond):
    sectors, rows, cols = wavefunction.shape
    terms = left_env.shape[1]
    nsec = lax.axis_size("sec")
    kernel, near, zs, wide, half = make_kernel(nsec, sectors, terms, rows, cols)
    vmem = pl.BlockSpec(memory_space=pltpu.VMEM)
    hbm = pl.BlockSpec(memory_space=pltpu.HBM)
    held = pltpu.VMEM((wide, ENV, rows, half), BF)
    field = pltpu.VMEM((sectors, rows, cols), F32)
    dma = pltpu.SemaphoreType.DMA
    vector, ritz = pl.pallas_call(
        kernel,
        out_shape=(
            jax.ShapeDtypeStruct((sectors, rows, cols), F32),
            jax.ShapeDtypeStruct((2, LANES), F32),
        ),
        in_specs=[hbm] * 6,
        out_specs=(vmem, vmem),
        scratch_shapes=[
            pltpu.SMEM(shifts.shape, jnp.int32),
            pltpu.SMEM((2, sectors), jnp.int32),
            pltpu.VMEM(wavefunction.shape, F32),
            pltpu.VMEM(precond.shape, F32),
            pltpu.VMEM(left_env.shape, BF),
            pltpu.VMEM(right_env.shape, BF),
            held, held, held, held, held, held, held, held,
            pltpu.VMEM((wide, ENV, 1, LANES), F32),
            pltpu.VMEM((LANES, LANES), F32),
            pltpu.VMEM((wide, ENV, rows, LANES), F32),
            pltpu.VMEM((sectors, rows, LANES), F32),
            field, field, field, field, field, field, field, field, field,
            pltpu.VMEM((3, near, 1, LANES), F32),
            pltpu.VMEM((3, zs, 1, LANES), F32),
            dma((6,)),
            dma((3, 2, ENV)), dma((3, 2, ENV)), dma((3, 2, ENV)), dma((3, 2, ENV)),
            dma((3, 2, 4, ENV)),
            dma((3, ENV)), dma((3, ENV)),
            dma((3,)), dma((3,)), dma((3,)), dma((3,)),
            pltpu.SemaphoreType.REGULAR((2,)),
        ],
        compiler_params=pltpu.CompilerParams(
            collective_id=0, has_side_effects=True, vmem_limit_bytes=40 << 20
        ),
    )(*(pltpu.with_memory_space_constraint(a, pltpu.HBM) for a in (shifts, block_dims.T, wavefunction, precond, left_env, right_env)))
    return vector, ritz[:, 0]


def solution(mesh):
    in_specs = (
        P("sec", "env", None),
        P("sec", None, "env", None),
        P("sec", None, None, None),
        P(),
        P("sec", None),
        P("sec", "env"),
    )
    out_specs = (P("sec", "env", None), P())
    return jax.shard_map(local, mesh=mesh, in_specs=in_specs, out_specs=out_specs, check_vma=False)
```
